512 devices in a mesh: seq: 32 (over x, y, core), key: 16 (over z).
Axes of the slice: x: 4, y: 4, z: 16, core: 2. Of those that a mesh axis runs over, the one named last changes fastest.
Arguments:
- query_rows: bfloat16 [8192, 16, 256], P('seq', None, 'key'), may hold values from -0.375 to 0.375
- key_rows: bfloat16 [8192, 16, 256], P('seq', None, 'key'), may hold values from -0.1875 to 0.1875
- value_rows: bfloat16 [8192, 16, 256], P('seq', 'key'), may hold values from -6 to 6
- out_grad: bfloat16 [8192, 16, 256], P('seq', 'key')
- log_gates: float32 [16, 8192], P('key', 'seq'), may hold values from -0.8 to 0, as said below
- write_rate: float32 [16, 8192], P('key', 'seq'), may hold values from 0.1 to 0.8
- group_inverse: bfloat16 [64, 16, 128, 128], P('seq', 'key'), as said below
- states: bfloat16 [64, 16, 256, 256], P('seq', None, 'key'), may hold values from -0.75 to 0.75
Outputs:
- grad_query: bfloat16 [8192, 16, 256], P('seq', None, 'key')
- grad_key: bfloat16 [8192, 16, 256], P('seq', None, 'key')
- grad_value: bfloat16 [8192, 16, 256], P('seq', 'key')
- grad_square: float32 [], replicated
The draws below stay inside these ranges and needn't reach their ends.
Inputs may be any that keep to these rules, and one draw needn't show every extreme that they name: `group_inverse`: each group's matrix is unit lower triangular: ones on the diagonal, zeros above it. `log_gates`: every entry is the logarithm of a decay factor, never positive.
All inputs are finite; a program needn't handle non-finite values.
Results may differ from the reference program's by a relative error of at most 0.007.
Values may be sent and summed in bfloat16 or wider, within the bound.
No kernel may reach another device: no remote copies, remote signals or barrier semaphores. Data moves between devices by JAX's collectives and lax.ppermute only.
A program may use at most 128 MiB of HBM per device.

```python
import math
import jax
import jax.numpy as jnp
from jax import lax

HEAD_COUNT = 16
KD = 256
VD = 256
GROUP = 128
TOK_DEV = 256
GROUPS = 64
SEQUENCE_TOKENS = 8192
N_SEQ = 32


def draw_out_grad(key, part):
    shape = (SEQUENCE_TOKENS, HEAD_COUNT, VD)
    base = jnp.clip(jax.random.normal(key, shape, jnp.float32), -5.0, 5.0)
    rising = jnp.exp(jnp.arange(SEQUENCE_TOKENS, dtype=jnp.float32) * (math.log(3.0) / SEQUENCE_TOKENS))
    return (base * rising[:, None, None]).astype(jnp.bfloat16)


def draw_log_gates(key, part):
    every_key_row = jax.random.split(key, 5)
    low_rate = math.log(0.3 / SEQUENCE_TOKENS)
    high_rate = math.log(0.03)
    per_head_rate = jnp.exp(jax.random.uniform(every_key_row[0], (HEAD_COUNT, 1), jnp.float32, low_rate, high_rate))
    block_multiplier = jnp.exp(jax.random.uniform(every_key_row[1], (1, N_SEQ), jnp.float32, math.log(0.6), math.log(1.6)))
    block_multiplier = jnp.repeat(block_multiplier, TOK_DEV, axis=1)
    token_multiplier = jax.random.uniform(every_key_row[2], (HEAD_COUNT, SEQUENCE_TOKENS), jnp.float32, 0.5, 1.5)
    spike_positions_list = jax.random.randint(every_key_row[3], (HEAD_COUNT, 2), 0, SEQUENCE_TOKENS)
    locations = jnp.arange(SEQUENCE_TOKENS)[None, None, :] == spike_positions_list[:, :, None]
    spike_mask = jnp.any(locations, axis=1)
    spike_length = jnp.log(jax.random.uniform(every_key_row[4], (HEAD_COUNT, SEQUENCE_TOKENS), jnp.float32, 0.5, 0.8))
    return -per_head_rate * block_multiplier * token_multiplier + jnp.where(spike_mask, spike_length, 0.0)


def draw_group_inverse(key, part):
    shape = (GROUPS, HEAD_COUNT, GROUP, GROUP)
    row_ids = jnp.arange(GROUP)[:, None]
    col_ids = jnp.arange(GROUP)[None, :]
    noise = jnp.clip(jax.random.normal(key, shape, jnp.float32), -4.0, 4.0)
    scaled = noise * (0.25 / math.sqrt(GROUP))
    return (jnp.where(row_ids > col_ids, scaled, 0.0) + jnp.where(row_ids == col_ids, 1.0, 0.0)).astype(jnp.bfloat16)


def level_of(stream_key, shape, cuts, smallest, high):
    def one(position, blocks):
        heights = jax.random.uniform(jax.random.fold_in(jax.random.fold_in(stream_key, 6), position), (blocks,), jnp.float32, smallest / len(cuts), high / len(cuts))
        return jnp.repeat(jnp.exp(heights), shape[position] // blocks).reshape((-1,) + (1,) * (len(shape) - position - 1))

    factor_of = one(*cuts[0])
    for cut in cuts[1:]:
        factor_of = factor_of * one(*cut)
    return factor_of


def scatter_about(key, dims, scale, most, shards=(), kind=jnp.bfloat16):
    entries = jax.random.normal(key, dims, jnp.float32) * scale
    if len(shards) > 0:
        entries = level_of(key, dims, shards, -0.22, 0.18) * entries
    return jnp.clip(entries, min=-most, max=most).astype(kind)


def setup_inputs(seed: int = 0) -> dict:
    key_list = jax.random.split(jax.random.key(seed), 9)
    return {
        "query_rows": scatter_about(key_list[0], (SEQUENCE_TOKENS, HEAD_COUNT, KD), KD ** -0.5, 0.375, ((0, 32), (2, 16))),
        "key_rows": scatter_about(key_list[1], (SEQUENCE_TOKENS, HEAD_COUNT, KD), (4 * KD) ** -0.5, 0.1875, ((0, 32), (2, 16))),
        "value_rows": scatter_about(key_list[2], (SEQUENCE_TOKENS, HEAD_COUNT, VD), 1.0, 6.0, ((0, 32), (1, 16))),
        "out_grad": draw_out_grad(jax.random.fold_in(key_list[8], 71), 0),
        "log_gates": draw_log_gates(jax.random.fold_in(key_list[8], 71), 0),
        "write_rate": jnp.clip(0.1 + 0.7 * jax.random.uniform(key_list[5], (HEAD_COUNT, SEQUENCE_TOKENS), jnp.float32) ** level_of(key_list[5], (HEAD_COUNT, SEQUENCE_TOKENS), ((0, 16), (1, 32)), -0.2, 0.2), 0.1, 0.8),
        "group_inverse": draw_group_inverse(jax.random.fold_in(key_list[8], 71), 0),
        "states": scatter_about(key_list[7], (GROUPS, HEAD_COUNT, KD, VD), (VD // 4) ** -0.5, 0.75, ((0, 32), (2, 16))),
    }


def precise_product(form, left, right):
    return jnp.einsum(form, left.astype(jnp.float32), right.astype(jnp.float32), precision=lax.Precision.HIGHEST)


def token_wise(factor):
    return jnp.transpose(factor)[:, :, None]


def square_sum(array):
    return jnp.sum(jnp.square(array.astype(jnp.float32)))


def reference(query_rows, key_rows, value_rows, out_grad, log_gates, write_rate, group_inverse, states):
    halfway_point = jnp.bfloat16
    query_all = query_rows.reshape(GROUPS, GROUP, HEAD_COUNT, KD)
    key_all = key_rows.reshape(GROUPS, GROUP, HEAD_COUNT, KD)
    value_all = value_rows.reshape(GROUPS, GROUP, HEAD_COUNT, VD)
    grad_all = out_grad.reshape(GROUPS, GROUP, HEAD_COUNT, VD)
    gate_all = jnp.transpose(log_gates.reshape(HEAD_COUNT, GROUPS, GROUP), (1, 0, 2))
    rate_all = jnp.transpose(write_rate.reshape(HEAD_COUNT, GROUPS, GROUP), (1, 0, 2))
    row_ids = jnp.arange(GROUP)[:, None]
    col_ids = jnp.arange(GROUP)[None, :]
    lower = row_ids >= col_ids

    def group_back(state_gradient, pieces):
        group_queries, group_keys, value_c, group_gradient, gate_c, group_rates, group_inverse_matrix, group_state = pieces
        gamma = jnp.cumsum(gate_c, axis=1)
        final_gamma_value = gamma[:, -1:]
        incoming_decay = jnp.exp(gamma)
        outgoing_decay = jnp.exp(final_gamma_value - gamma)
        spread = gamma[:, :, None] - gamma[:, None, :]
        decay_mask = jnp.where(lower, jnp.exp(jnp.where(lower, spread, 0.0)), 0.0)
        key_scaled = (group_keys * token_wise(group_rates * incoming_decay)).astype(halfway_point)
        written_keys = precise_product("xzw,wxa->zxa", group_inverse_matrix, key_scaled).astype(halfway_point)
        scaled_values = (value_c * token_wise(group_rates)).astype(halfway_point)
        fresh_values = (precise_product("fed,dfp->efp", group_inverse_matrix, scaled_values) - precise_product("sid,idb->sib", written_keys, group_state)).astype(halfway_point)
        score_mat = (precise_product("thk,shk->hts", group_queries, group_keys) * decay_mask).astype(halfway_point)
        key_result = (group_keys * token_wise(outgoing_decay)).astype(halfway_point)
        incoming_query = (group_queries * token_wise(incoming_decay)).astype(halfway_point)
        inner_gradient = precise_product("hts,thv->shv", score_mat, group_gradient)
        value_gradient = inner_gradient + precise_product("sid,idb->sib", key_result, state_gradient)
        previous_state = jnp.exp(final_gamma_value)[:, :, None] * state_gradient + precise_product("nwf,nwo->wfo", incoming_query, group_gradient) - precise_product("nwf,nwo->wfo", written_keys, value_gradient)
        value_rounding = value_gradient.astype(halfway_point)
        grad_value_c = (token_wise(group_rates) * precise_product("hts,thv->shv", group_inverse_matrix, value_rounding)).astype(halfway_point)
        score_gradient = (precise_product("thv,shv->hts", group_gradient, fresh_values) * decay_mask).astype(halfway_point)
        write_gradient = (-precise_product("lgr,gwr->lgw", value_rounding, group_state)).astype(halfway_point)
        state_rounding = state_gradient.astype(halfway_point)
        group_query_gradient = (token_wise(incoming_decay) * precise_product("lgr,gwr->lgw", group_gradient, group_state) + precise_product("xzw,wxa->zxa", score_gradient, group_keys)).astype(halfway_point)
        group_key_gradient = (precise_product("xfp,fxz->pxz", score_gradient, group_queries) + token_wise(outgoing_decay) * precise_product("lgr,gwr->lgw", fresh_values, state_rounding) + token_wise(group_rates * incoming_decay) * precise_product("xfp,fxz->pxz", group_inverse_matrix, write_gradient)).astype(halfway_point)
        return previous_state, (group_query_gradient, group_key_gradient, grad_value_c)

    final_grad = jnp.zeros((HEAD_COUNT, KD, VD), jnp.float32)
    pieces = (query_all, key_all, value_all, grad_all, gate_all, rate_all, group_inverse, states)
    _, outputs = lax.scan(group_back, final_grad, pieces, reverse=True)
    grad_query = outputs[0].reshape(SEQUENCE_TOKENS, HEAD_COUNT, KD)
    grad_key = outputs[1].reshape(SEQUENCE_TOKENS, HEAD_COUNT, KD)
    grad_value = outputs[2].reshape(SEQUENCE_TOKENS, HEAD_COUNT, VD)
    summed = square_sum(grad_query) + square_sum(grad_key) + square_sum(grad_value)
    grad_square = summed / (SEQUENCE_TOKENS * HEAD_COUNT * (2 * KD + VD))
    return grad_query, grad_key, grad_value, grad_square
```

```python
import jax
import jax.numpy as jnp
from jax import lax
from jax.experimental import pallas as pl
from jax.experimental.pallas import tpu as pltpu
from jax.sharding import Mesh, PartitionSpec as P

F32 = jnp.float32
BF16 = jnp.bfloat16
SEQ = ("x", "y", "c")
N = 128
K = 256
V = 256
W2 = K + V
PAD = 16


def nn(a, b):
    return lax.dot_general(a, b, (((1,), (0,)), ((), ())), preferred_element_type=F32)


def nt(a, b):
    return lax.dot_general(a, b, (((1,), (1,)), ((), ())), preferred_element_type=F32)


def tn(a, b):
    return lax.dot_general(a, b, (((0,), (0,)), ((), ())), preferred_element_type=F32)


def split(a):
    high = a.astype(BF16)
    return high, (a - high.astype(F32)).astype(BF16)


def nn2(a, b):
    high, low = split(b)
    return nn(a, high) + nn(a, low)


def tn2(a, b):
    high, low = split(b)
    return tn(a, high) + tn(a, low)


def gates_of(gate_row, rate_row):
    rows = lax.broadcasted_iota(jnp.int32, (N, N), 0)
    cols = lax.broadcasted_iota(jnp.int32, (N, N), 1)
    lower = cols <= rows
    eye = cols == rows
    gate_col = jnp.sum(jnp.where(eye, gate_row, 0.0), axis=1, keepdims=True)
    rate_col = jnp.sum(jnp.where(eye, rate_row, 0.0), axis=1, keepdims=True)
    gamma_col = jnp.sum(jnp.where(lower, gate_row, 0.0), axis=1, keepdims=True)
    gamma_row = jnp.sum(jnp.where(rows <= cols, gate_col, 0.0), axis=0, keepdims=True)
    gamma_end = jnp.sum(gate_row, axis=1, keepdims=True)
    spread = jnp.where(lower, gamma_col - gamma_row, 0.0)
    mask = jnp.where(lower, jnp.exp(spread), 0.0)
    return gamma_row, gamma_end, mask, rate_col


def compose(first, second):
    decay1, m1, b1 = first
    decay2, m2, b2 = second
    both = nn(m1.astype(BF16), jnp.concatenate([m2, b2], axis=1).astype(BF16))
    return decay1 * decay2, decay2 * m1 + decay1 * m2 - both[:, :K], decay1 * b2 + b1 - both[:, K:]


def decay_rows(decay):
    high = decay.astype(BF16).astype(F32)
    middle = (decay - high).astype(BF16).astype(F32)
    low = decay - high - middle
    rows = lax.broadcasted_iota(jnp.int32, (PAD, W2), 0)
    return jnp.where(rows == 0, high, jnp.where(rows == 1, middle, jnp.where(rows == 2, low, 0.0))).astype(BF16)


def decay_from(block):
    return jnp.sum(block.astype(F32), axis=0, keepdims=True)[:, :1]


def unpack(block):
    return decay_from(block[K:]), block[:K, :K].astype(F32), block[:K, K:].astype(F32)


def unpack_halves(low, high):
    body = jnp.concatenate([low[: K // 2], high[: K // 2]], axis=0)
    return decay_from(low[K // 2 :]), body[:, :K].astype(F32), body[:, K:].astype(F32)


def head_rows(kq_ref, which):
    return kq_ref[:, 16 * which : 16 * which + 16, :].reshape(K, 2 * N)


def local_map_kernel(kq_ref, grad_ref, gate_ref, rate_ref, inv_ref, map_ref, wt_ref, lg_ref):
    key_t = head_rows(kq_ref, 0)
    query_t = head_rows(kq_ref, 1)
    maps = []
    for g in range(2):
        span = slice(g * N, (g + 1) * N)
        rate = rate_ref[:, span]
        gamma, gamma_end, mask, _ = gates_of(gate_ref[:, span], rate)
        kt, qt = key_t[:, span], query_t[:, span]
        into = jnp.exp(gamma)
        scaled = (kt * (rate * into)).astype(BF16)
        wt = nt(scaled, inv_ref[g, 0]).astype(BF16)
        wt_ref[:, span] = wt
        score = (tn(qt, kt) * mask).astype(BF16)
        out_t = (kt * jnp.exp(gamma_end - gamma)).astype(BF16)
        in_t = (qt * into).astype(BF16)
        grad = grad_ref[span, :]
        lg = tn(score, grad)
        lg_ref[span, :] = lg
        offset = nn(in_t, grad) - nn2(wt, lg)
        maps.append((jnp.exp(gamma_end), nt(wt, out_t), offset))
    decay, m, b = compose(*maps)
    map_ref[:K, :K] = m.astype(BF16)
    map_ref[:K, K:] = b.astype(BF16)
    map_ref[K:, :] = decay_rows(decay)


def pair_kernel(place_ref, pair_ref, half_ref, full_ref):
    decay, m, b = compose(unpack(pair_ref[0]), unpack(pair_ref[1]))
    full_ref[:K, :K] = m.astype(BF16)
    full_ref[:K, K:] = b.astype(BF16)
    rows = decay_rows(decay)
    full_ref[K:, :] = rows
    half_ref[K // 2 :, :] = rows
    half_ref[: K // 2, :] = full_ref[pl.ds(pl.multiple_of(place_ref[1] * (K // 2), K // 2), K // 2), :]


def plane_kernel(place_ref, pair_ref, own_ref, halves_ref, half_ref, em_ref, eb_ref, slots, body, ends):
    y, c = place_ref[0], place_ref[1]
    slots[y] = own_ref[...]
    for d in range(1, 4):
        at = lax.rem(y + d, 4)
        slots[at, : K // 2, :] = halves_ref[0, d - 1, : K // 2, :]
        slots[at, K // 2 : K, :] = halves_ref[1, d - 1, : K // 2, :]
        slots[at, K:, :] = halves_ref[0, d - 1, K // 2 :, :]
    suffix = unpack(slots[3])
    end = (jnp.ones((1, 1), F32), jnp.zeros((K, K), F32), jnp.zeros((K, V), F32))
    for j in (2, 1, 0):
        here = y == j
        end = tuple(jnp.where(here, s, e) for s, e in zip(suffix, end))
        suffix = compose(unpack(slots[j]), suffix)
    decay, m, b = suffix
    body[:, :K] = m.astype(BF16)
    body[:, K:] = b.astype(BF16)
    half_ref[K // 2 :, :] = decay_rows(decay)
    half_ref[: K // 2, :] = body[pl.ds(pl.multiple_of(c * (K // 2), K // 2), K // 2), :]
    inner = compose(unpack(pair_ref[1]), end)
    decay, m, b = tuple(jnp.where(c == 0, i, e) for i, e in zip(inner, end))
    em_ref[...] = m.astype(BF16)
    eb_ref[:K, :] = b
    eb_ref[K:, :] = jnp.broadcast_to(decay, (8, V))


def ahead_kernel(kq_ref, grad_ref, gate_ref, rate_ref, inv_ref, wt_ref, value_ref, state_ref,
                 gq_ref, nv_ref, ct_ref, sum_ref):
    key_t = head_rows(kq_ref, 0)
    query_t = head_rows(kq_ref, 1)
    total = jnp.zeros((1, 1), F32)
    for g in range(2):
        span = slice(g * N, (g + 1) * N)
        gamma, _, mask, rate_col = gates_of(gate_ref[:, span], rate_ref[:, span])
        kt, qt = key_t[:, span], query_t[:, span]
        state = state_ref[:, g].reshape(K, V)
        grad = grad_ref[span, :]
        scaled = (value_ref[span, :] * rate_col).astype(BF16)
        fresh = (nn(inv_ref[g, 0], scaled) - tn(wt_ref[:, span], state)).astype(BF16)
        nv_ref[span, :] = fresh
        score = (nt(grad, fresh) * mask).astype(BF16)
        gq = (jnp.exp(gamma) * nt(state, grad) + nt(kt, score)).astype(BF16)
        gq_ref[:, :, span] = gq.reshape(16, 16, N)
        ct_ref[:, span] = nn(qt, score)
        total += jnp.sum(jnp.square(gq.astype(F32)), keepdims=True)
    sum_ref[...] = jnp.broadcast_to(total, (8, 128))


def final_kernel(halves_ref, em_ref, eb_ref, kq_ref, grad_ref, gate_ref, rate_ref, inv_ref, wt_ref, lg_ref,
                 state_ref, nv_ref, ct_ref, sum_ref, gk_ref, gv_ref):
    key_t = head_rows(kq_ref, 0)
    query_t = head_rows(kq_ref, 1)
    later = None
    for d in (2, 1, 0):
        decay, m, b = unpack_halves(halves_ref[0, d], halves_ref[1, d])
        later = b if later is None else decay * later + b - nn(m.astype(BF16), later.astype(BF16))
    state_grad = eb_ref[K : K + 1, :1] * later + eb_ref[:K, :] - nn(em_ref[...], later.astype(BF16))
    total = sum_ref[:1, :1]
    for g in (1, 0):
        span = slice(g * N, (g + 1) * N)
        rate = rate_ref[:, span]
        gamma, gamma_end, _, rate_col = gates_of(gate_ref[:, span], rate)
        into = jnp.exp(gamma)
        away = jnp.exp(gamma_end - gamma)
        inverse = inv_ref[g, 0]
        out_t = (key_t[:, span] * away).astype(BF16)
        high, low = split(state_grad)
        value_grad = lg_ref[span, :] + tn(out_t, high) + tn(out_t, low)
        rounded = value_grad.astype(BF16)
        gv = (rate_col * tn(inverse, rounded)).astype(BF16)
        gv_ref[span, :] = gv
        write_t = (-nt(state_ref[:, g].reshape(K, V), rounded)).astype(BF16)
        gk = (ct_ref[:, span] + away * nt(high, nv_ref[span, :]) + (rate * into) * nn(write_t, inverse)).astype(BF16)
        gk_ref[:, :, span] = gk.reshape(16, 16, N)
        total += jnp.sum(jnp.square(gk.astype(F32)), keepdims=True) + jnp.sum(
            jnp.square(gv.astype(F32)), keepdims=True
        )
        if g == 1:
            in_t = (query_t[:, span] * into).astype(BF16)
            state_grad = (
                jnp.exp(gamma_end) * state_grad
                + nn(in_t, grad_ref[span, :])
                - nn2(wt_ref[:, span], value_grad)
            )
    high = total.astype(BF16).astype(F32)
    middle = (total - high).astype(BF16).astype(F32)
    low = total - high - middle
    rows = lax.broadcasted_iota(jnp.int32, (16, 128), 0)
    pieces = jnp.where(rows == 0, high, jnp.where(rows == 1, middle, jnp.where(rows == 2, low, 0.0)))
    gk_ref[:, :, 2 * N :] = jnp.broadcast_to(pieces.astype(BF16)[None], (16, 16, 128))


def call(kernel, outs, args, flops, scratch=(), scalars=0):
    spec = pl.BlockSpec(memory_space=pltpu.VMEM)
    smem = pl.BlockSpec(memory_space=pltpu.SMEM)
    moved = sum(a.size * a.dtype.itemsize for a in args)
    return pl.pallas_call(
        kernel,
        out_shape=outs,
        in_specs=[smem] * scalars + [spec] * (len(args) - scalars),
        out_specs=[spec] * len(outs),
        scratch_shapes=list(scratch),
        cost_estimate=pl.CostEstimate(flops=flops, bytes_accessed=moved, transcendentals=0),
        compiler_params=pltpu.CompilerParams(vmem_limit_bytes=24 * 2**20),
    )(*args)


def shape(dims, dtype=BF16):
    return jax.ShapeDtypeStruct(dims, dtype)


def to_heads(array):
    return lax.all_to_all(array, "key", 0, 0, tiled=True)


def local(query_rows, key_rows, value_rows, out_grad, log_gates, write_rate, group_inverse, states):
    keys = jnp.transpose(key_rows, (1, 2, 0))
    queries = jnp.transpose(query_rows, (1, 2, 0))
    kq = to_heads(jnp.concatenate([keys, queries], axis=1))
    grad = out_grad.reshape(2 * N, V)
    values = value_rows.reshape(2 * N, V)
    place = jnp.stack([lax.axis_index("y"), lax.axis_index("c")]).astype(jnp.int32)
    half = shape((K // 2 + PAD, W2))
    full = shape((K + PAD, W2))
    square = shape((K, V), F32)
    basics = (kq, grad, log_gates, write_rate, group_inverse)

    device_map, written_t, local_grad = call(
        local_map_kernel, [full, shape((K, 2 * N)), square], basics, 10**8
    )
    pair = lax.all_gather(device_map, "c")
    pair_half, pair_full = call(pair_kernel, [half, full], (place, pair), 10**8, scalars=1)
    state_blocks = jnp.transpose(states, (1, 0, 2, 3))
    state_blocks, pair_half = lax.optimization_barrier((state_blocks, pair_half))
    state_heads = to_heads(state_blocks)
    around = [
        lax.ppermute(pair_half, "y", [(s, (s - d) % 4) for s in range(4)]) for d in (1, 2, 3)
    ]
    pair_halves = lax.all_gather(jnp.stack(around), "c")
    plane_half, end_m, end_b = call(
        plane_kernel,
        [half, shape((K, K)), shape((K + 8, V), F32)],
        (place, pair, pair_full, pair_halves),
        5 * 10**8,
        scratch=[pltpu.VMEM((4, K + PAD, W2), BF16), pltpu.VMEM((K, W2), BF16), pltpu.VMEM((8, 128), F32)],
        scalars=1,
    )
    later = [lax.ppermute(plane_half, "x", [(s, s - d) for s in range(d, 4)]) for d in (1, 2, 3)]
    plane_halves = lax.all_gather(jnp.stack(later), "c")

    gq, fresh, score_term, query_sum = call(
        ahead_kernel,
        [shape((16, 16, 2 * N)), shape((2 * N, V)), square, shape((8, 128), F32)],
        (*basics, written_t, values, state_heads),
        2 * 10**8,
    )
    grad_query = to_heads(gq)
    gk, grad_value = call(
        final_kernel,
        [shape((16, 16, 3 * N)), shape((2 * N, V))],
        (plane_halves, end_m, end_b, *basics, written_t, local_grad, state_heads, fresh, score_term, query_sum),
        4 * 10**8,
    )
    gk = to_heads(gk)
    part = jnp.sum(gk[:, :3, 2 * N].astype(F32))
    parts = lax.all_to_all(jnp.full((32, 1, 128), part), SEQ, 0, 0, tiled=True)
    grad_square = jnp.sum(parts[:, 0, 0]) / (8192 * 16 * (2 * K + V))
    grad_key = jnp.transpose(gk[:, :, : 2 * N], (2, 0, 1))
    return (
        jnp.transpose(grad_query, (2, 0, 1)),
        grad_key,
        grad_value.reshape(2 * N, 1, V),
        grad_square,
    )


def solution(mesh):
    grid = Mesh(mesh.devices.reshape(4, 4, 2, 16), ("x", "y", "c", "key"))
    in_specs = (
        P(SEQ, None, "key"),
        P(SEQ, None, "key"),
        P(SEQ, "key", None),
        P(SEQ, "key", None),
        P("key", SEQ),
        P("key", SEQ),
        P(SEQ, "key", None, None),
        P(SEQ, None, "key", None),
    )
    out_specs = (P(SEQ, None, "key"), P(SEQ, None, "key"), P(SEQ, "key", None), P())
    return jax.shard_map(local, mesh=grid, in_specs=in_specs, out_specs=out_specs, check_vma=False)
```

```python
import jax
import jax.numpy as jnp
from jax import lax
from jax.experimental import pallas as pl
from jax.experimental.pallas import tpu as pltpu
from jax.sharding import Mesh, PartitionSpec as P

F32 = jnp.float32
BF16 = jnp.bfloat16
SEQ = ("x", "y", "c")
N = 128
K = 256
V = 256
W2 = K + V
PAD = 16


def nn(a, b):
    return lax.dot_general(a, b, (((1,), (0,)), ((), ())), preferred_element_type=F32)


def nt(a, b):
    return lax.dot_general(a, b, (((1,), (1,)), ((), ())), preferred_element_type=F32)


def tn(a, b):
    return lax.dot_general(a, b, (((0,), (0,)), ((), ())), preferred_element_type=F32)


def split(a):
    high = a.astype(BF16)
    return high, (a - high.astype(F32)).astype(BF16)


def nn2(a, b):
    high, low = split(b)
    return nn(a, high) + nn(a, low)


def tn2(a, b):
    high, low = split(b)
    return tn(a, high) + tn(a, low)


def gates_of(gate_row, rate_row):
    rows = lax.broadcasted_iota(jnp.int32, (N, N), 0)
    cols = lax.broadcasted_iota(jnp.int32, (N, N), 1)
    lower = cols <= rows
    eye = cols == rows
    gate_col = jnp.sum(jnp.where(eye, gate_row, 0.0), axis=1, keepdims=True)
    rate_col = jnp.sum(jnp.where(eye, rate_row, 0.0), axis=1, keepdims=True)
    gamma_col = jnp.sum(jnp.where(lower, gate_row, 0.0), axis=1, keepdims=True)
    gamma_row = jnp.sum(jnp.where(rows <= cols, gate_col, 0.0), axis=0, keepdims=True)
    gamma_end = jnp.sum(gate_row, axis=1, keepdims=True)
    spread = jnp.where(lower, gamma_col - gamma_row, 0.0)
    mask = jnp.where(lower, jnp.exp(spread), 0.0)
    return gamma_row, gamma_end, mask, rate_col


def compose(first, second):
    decay1, m1, b1 = first
    decay2, m2, b2 = second
    both = nn(m1.astype(BF16), jnp.concatenate([m2, b2], axis=1).astype(BF16))
    return decay1 * decay2, decay2 * m1 + decay1 * m2 - both[:, :K], decay1 * b2 + b1 - both[:, K:]


def decay_rows(decay):
    high = decay.astype(BF16).astype(F32)
    middle = (decay - high).astype(BF16).astype(F32)
    low = decay - high - middle
    rows = lax.broadcasted_iota(jnp.int32, (PAD, W2), 0)
    return jnp.where(rows == 0, high, jnp.where(rows == 1, middle, jnp.where(rows == 2, low, 0.0))).astype(BF16)


def decay_from(block):
    return jnp.sum(block.astype(F32), axis=0, keepdims=True)[:, :1]


def unpack(block):
    return decay_from(block[K:]), block[:K, :K].astype(F32), block[:K, K:].astype(F32)


def unpack_halves(low, high):
    body = jnp.concatenate([low[: K // 2], high[: K // 2]], axis=0)
    return decay_from(low[K // 2 :]), body[:, :K].astype(F32), body[:, K:].astype(F32)


def head_rows(kq_ref, which):
    return kq_ref[:, 16 * which : 16 * which + 16, :].reshape(K, 2 * N)


def local_map_kernel(kq_ref, grad_ref, gate_ref, rate_ref, inv_ref, map_ref, wt_ref, lg_ref):
    key_t = head_rows(kq_ref, 0)
    query_t = head_rows(kq_ref, 1)
    maps = []
    for g in range(2):
        span = slice(g * N, (g + 1) * N)
        rate = rate_ref[:, span]
        gamma, gamma_end, mask, _ = gates_of(gate_ref[:, span], rate)
        kt, qt = key_t[:, span], query_t[:, span]
        into = jnp.exp(gamma)
        scaled = (kt * (rate * into)).astype(BF16)
        wt = nt(scaled, inv_ref[g, 0]).astype(BF16)
        wt_ref[:, span] = wt
        score = (tn(qt, kt) * mask).astype(BF16)
        out_t = (kt * jnp.exp(gamma_end - gamma)).astype(BF16)
        in_t = (qt * into).astype(BF16)
        grad = grad_ref[span, :]
        lg = tn(score, grad)
        lg_ref[span, :] = lg
        offset = nn(in_t, grad) - nn2(wt, lg)
        maps.append((jnp.exp(gamma_end), nt(wt, out_t), offset))
    decay, m, b = compose(*maps)
    map_ref[:K, :K] = m.astype(BF16)
    map_ref[:K, K:] = b.astype(BF16)
    map_ref[K:, :] = decay_rows(decay)


def pair_kernel(place_ref, pair_ref, half_ref, full_ref):
    decay, m, b = compose(unpack(pair_ref[0]), unpack(pair_ref[1]))
    full_ref[:K, :K] = m.astype(BF16)
    full_ref[:K, K:] = b.astype(BF16)
    rows = decay_rows(decay)
    full_ref[K:, :] = rows
    half_ref[K // 2 :, :] = rows
    half_ref[: K // 2, :] = full_ref[pl.ds(pl.multiple_of(place_ref[1] * (K // 2), K // 2), K // 2), :]


def plane_kernel(place_ref, pair_ref, own_ref, halves_ref, half_ref, em_ref, eb_ref, slots, body, ends):
    y, c = place_ref[0], place_ref[1]
    slots[y] = own_ref[...]
    for d in range(1, 4):
        at = lax.rem(y + d, 4)
        slots[at, : K // 2, :] = halves_ref[0, d - 1, : K // 2, :]
        slots[at, K // 2 : K, :] = halves_ref[1, d - 1, : K // 2, :]
        slots[at, K:, :] = halves_ref[0, d - 1, K // 2 :, :]
    suffix = unpack(slots[3])
    end = (jnp.ones((1, 1), F32), jnp.zeros((K, K), F32), jnp.zeros((K, V), F32))
    for j in (2, 1, 0):
        here = y == j
        end = tuple(jnp.where(here, s, e) for s, e in zip(suffix, end))
        suffix = compose(unpack(slots[j]), suffix)
    decay, m, b = suffix
    body[:, :K] = m.astype(BF16)
    body[:, K:] = b.astype(BF16)
    half_ref[K // 2 :, :] = decay_rows(decay)
    half_ref[: K // 2, :] = body[pl.ds(pl.multiple_of(c * (K // 2), K // 2), K // 2), :]
    inner = compose(unpack(pair_ref[1]), end)
    decay, m, b = tuple(jnp.where(c == 0, i, e) for i, e in zip(inner, end))
    em_ref[...] = m.astype(BF16)
    eb_ref[:K, :] = b
    eb_ref[K:, :] = jnp.broadcast_to(decay, (8, V))


def ahead_kernel(kq_ref, grad_ref, gate_ref, rate_ref, inv_ref, wt_ref, value_ref, state_ref,
                 gq_ref, nv_ref, ct_ref, sum_ref):
    key_t = head_rows(kq_ref, 0)
    query_t = head_rows(kq_ref, 1)
    total = jnp.zeros((1, 1), F32)
    for g in range(2):
        span = slice(g * N, (g + 1) * N)
        gamma, _, mask, rate_col = gates_of(gate_ref[:, span], rate_ref[:, span])
        kt, qt = key_t[:, span], query_t[:, span]
        state = state_ref[:, g].reshape(K, V)
        grad = grad_ref[span, :]
        scaled = (value_ref[span, :] * rate_col).astype(BF16)
        fresh = (nn(inv_ref[g, 0], scaled) - tn(wt_ref[:, span], state)).astype(BF16)
        nv_ref[span, :] = fresh
        score = (nt(grad, fresh) * mask).astype(BF16)
        gq = (jnp.exp(gamma) * nt(state, grad) + nt(kt, score)).astype(BF16)
        gq_ref[:, :, span] = gq.reshape(16, 16, N)
        ct_ref[:, span] = nn(qt, score)
        total += jnp.sum(jnp.square(gq.astype(F32)), keepdims=True)
    sum_ref[...] = jnp.broadcast_to(total, (8, 128))


def final_kernel(halves_ref, em_ref, eb_ref, kq_ref, grad_ref, gate_ref, rate_ref, inv_ref, wt_ref, lg_ref,
                 state_ref, nv_ref, ct_ref, sum_ref, gq_ref, out_ref, gv_ref):
    key_t = head_rows(kq_ref, 0)
    query_t = head_rows(kq_ref, 1)
    later = None
    for d in (2, 1, 0):
        decay, m, b = unpack_halves(halves_ref[0, d], halves_ref[1, d])
        later = b if later is None else decay * later + b - nn(m.astype(BF16), later.astype(BF16))
    state_grad = eb_ref[K : K + 1, :1] * later + eb_ref[:K, :] - nn(em_ref[...], later.astype(BF16))
    total = sum_ref[:1, :1]
    out_ref[:, :16, :] = gq_ref[...]
    for g in (1, 0):
        span = slice(g * N, (g + 1) * N)
        rate = rate_ref[:, span]
        gamma, gamma_end, _, rate_col = gates_of(gate_ref[:, span], rate)
        into = jnp.exp(gamma)
        away = jnp.exp(gamma_end - gamma)
        inverse = inv_ref[g, 0]
        out_t = (key_t[:, span] * away).astype(BF16)
        high, low = split(state_grad)
        value_grad = lg_ref[span, :] + tn(out_t, high) + tn(out_t, low)
        rounded = value_grad.astype(BF16)
        gv = (rate_col * tn(inverse, rounded)).astype(BF16)
        gv_ref[span, :] = gv
        write_t = (-nt(state_ref[:, g].reshape(K, V), rounded)).astype(BF16)
        gk = (ct_ref[:, span] + away * nt(high, nv_ref[span, :]) + (rate * into) * nn(write_t, inverse)).astype(BF16)
        out_ref[:, 16:32, span] = gk.reshape(16, 16, N)
        total += jnp.sum(jnp.square(gk.astype(F32)), keepdims=True) + jnp.sum(
            jnp.square(gv.astype(F32)), keepdims=True
        )
        if g == 1:
            in_t = (query_t[:, span] * into).astype(BF16)
            state_grad = (
                jnp.exp(gamma_end) * state_grad
                + nn(in_t, grad_ref[span, :])
                - nn2(wt_ref[:, span], value_grad)
            )
    high = total.astype(BF16).astype(F32)
    middle = (total - high).astype(BF16).astype(F32)
    low = total - high - middle
    rows = lax.broadcasted_iota(jnp.int32, (8, 2 * N), 0)
    pieces = jnp.where(rows == 0, high, jnp.where(rows == 1, middle, jnp.where(rows == 2, low, 0.0)))
    out_ref[:, 32:, :] = jnp.broadcast_to(pieces.astype(BF16)[None], (16, 8, 2 * N))


def join_kernel(key_ref, query_ref, out_ref):
    out_ref[:, :16, :] = key_ref[...]
    out_ref[:, 16:, :] = query_ref[...]


def spread_kernel(back_ref, out_ref):
    pieces = jnp.sum(back_ref[:, 32:, :].astype(F32), axis=0)[:, :128]
    total = jnp.sum(pieces, axis=0, keepdims=True)
    out_ref[...] = jnp.broadcast_to(total[None], (32, 1, 128))


def call(kernel, outs, args, flops, scratch=(), scalars=0):
    spec = pl.BlockSpec(memory_space=pltpu.VMEM)
    smem = pl.BlockSpec(memory_space=pltpu.SMEM)
    moved = sum(a.size * a.dtype.itemsize for a in args)
    return pl.pallas_call(
        kernel,
        out_shape=outs,
        in_specs=[smem] * scalars + [spec] * (len(args) - scalars),
        out_specs=[spec] * len(outs),
        scratch_shapes=list(scratch),
        cost_estimate=pl.CostEstimate(flops=flops, bytes_accessed=moved, transcendentals=0),
        compiler_params=pltpu.CompilerParams(vmem_limit_bytes=24 * 2**20),
    )(*args)


def shape(dims, dtype=BF16):
    return jax.ShapeDtypeStruct(dims, dtype)


def to_heads(array):
    return lax.all_to_all(array, "key", 0, 0, tiled=True)


def local(query_rows, key_rows, value_rows, out_grad, log_gates, write_rate, group_inverse, states):
    keys = jnp.transpose(key_rows, (1, 2, 0))
    queries = jnp.transpose(query_rows, (1, 2, 0))
    (joined,) = call(join_kernel, [shape((16, 32, 2 * N))], (keys, queries), 0)
    kq = to_heads(joined)
    grad = out_grad.reshape(2 * N, V)
    values = value_rows.reshape(2 * N, V)
    place = jnp.stack([lax.axis_index("y"), lax.axis_index("c")]).astype(jnp.int32)
    half = shape((K // 2 + PAD, W2))
    full = shape((K + PAD, W2))
    square = shape((K, V), F32)
    basics = (kq, grad, log_gates, write_rate, group_inverse)

    device_map, written_t, local_grad = call(
        local_map_kernel, [full, shape((K, 2 * N)), square], basics, 10**8
    )
    pair = lax.all_gather(device_map, "c")
    pair_half, pair_full = call(pair_kernel, [half, full], (place, pair), 10**8, scalars=1)
    states, pair_half = lax.optimization_barrier((states, pair_half))
    state_heads = to_heads(jnp.transpose(states, (1, 0, 2, 3)))
    around = [
        lax.ppermute(pair_half, "y", [(s, (s - d) % 4) for s in range(4)]) for d in (1, 2, 3)
    ]
    pair_halves = lax.all_gather(jnp.stack(around), "c")
    plane_half, end_m, end_b = call(
        plane_kernel,
        [half, shape((K, K)), shape((K + 8, V), F32)],
        (place, pair, pair_full, pair_halves),
        6 * 10**10,
        scratch=[pltpu.VMEM((4, K + PAD, W2), BF16), pltpu.VMEM((K, W2), BF16), pltpu.VMEM((8, 128), F32)],
        scalars=1,
    )
    later = [lax.ppermute(plane_half, "x", [(s, s - d) for s in range(d, 4)]) for d in (1, 2, 3)]
    gq, fresh, score_term, query_sum = call(
        ahead_kernel,
        [shape((16, 16, 2 * N)), shape((2 * N, V)), square, shape((8, 128), F32)],
        (*basics, written_t, values, state_heads),
        2 * 10**8,
    )
    later, gq = lax.optimization_barrier((later, gq))
    plane_halves = lax.all_gather(jnp.stack(later), "c")
    gathered, grad_value = call(
        final_kernel,
        [shape((16, 40, 2 * N)), shape((2 * N, V))],
        (plane_halves, end_m, end_b, *basics, written_t, local_grad, state_heads, fresh, score_term, query_sum, gq),
        4 * 10**8,
    )
    back = to_heads(gathered)
    (spread,) = call(spread_kernel, [shape((32, 1, 128), F32)], (back,), 10**6)
    parts = lax.all_to_all(spread, SEQ, 0, 0, tiled=True)
    grad_square = jnp.sum(parts[:, 0, 0]) / (8192 * 16 * (2 * K + V))
    return (
        jnp.transpose(back[:, :16], (2, 0, 1)),
        jnp.transpose(back[:, 16:32], (2, 0, 1)),
        grad_value.reshape(2 * N, 1, V),
        grad_square,
    )


def solution(mesh):
    grid = Mesh(mesh.devices.reshape(4, 4, 2, 16), ("x", "y", "c", "key"))
    in_specs = (
        P(SEQ, None, "key"),
        P(SEQ, None, "key"),
        P(SEQ, "key", None),
        P(SEQ, "key", None),
        P("key", SEQ),
        P("key", SEQ),
        P(SEQ, "key", None, None),
        P(SEQ, None, "key", None),
    )
    out_specs = (P(SEQ, None, "key"), P(SEQ, None, "key"), P(SEQ, "key", None), P())
    return jax.shard_map(local, mesh=grid, in_specs=in_specs, out_specs=out_specs, check_vma=False)
```

```python
import jax
import jax.numpy as jnp
from jax import lax
from jax.experimental import pallas as pl
from jax.experimental.pallas import tpu as pltpu
from jax.sharding import Mesh, PartitionSpec as P

F32 = jnp.float32
BF16 = jnp.bfloat16
SEQ = ("x", "y", "c")
N = 128
K = 256
V = 256
HALF = V // 2
PAD = 16
PAIRS = [(0, 1), (1, 0), (2, 3), (3, 2)]
CROSS = [(0, 3), (3, 0), (1, 2), (2, 1)]
HIDING = 6 * 10**10


def nn(a, b):
    return lax.dot_general(a, b, (((1,), (0,)), ((), ())), preferred_element_type=F32)


def nt(a, b):
    return lax.dot_general(a, b, (((1,), (1,)), ((), ())), preferred_element_type=F32)


def tn(a, b):
    return lax.dot_general(a, b, (((0,), (0,)), ((), ())), preferred_element_type=F32)


def split(a):
    high = a.astype(BF16)
    return high, (a - high.astype(F32)).astype(BF16)


def nn2(a, b):
    high, low = split(b)
    return nn(a, high) + nn(a, low)


def tn2(a, b):
    high, low = split(b)
    return tn(a, high) + tn(a, low)


def gates_of(gate_row, rate_row):
    rows = lax.broadcasted_iota(jnp.int32, (N, N), 0)
    cols = lax.broadcasted_iota(jnp.int32, (N, N), 1)
    lower = cols <= rows
    eye = cols == rows
    gate_col = jnp.sum(jnp.where(eye, gate_row, 0.0), axis=1, keepdims=True)
    rate_col = jnp.sum(jnp.where(eye, rate_row, 0.0), axis=1, keepdims=True)
    gamma_col = jnp.sum(jnp.where(lower, gate_row, 0.0), axis=1, keepdims=True)
    gamma_row = jnp.sum(jnp.where(rows <= cols, gate_col, 0.0), axis=0, keepdims=True)
    gamma_end = jnp.sum(gate_row, axis=1, keepdims=True)
    spread = jnp.where(lower, gamma_col - gamma_row, 0.0)
    mask = jnp.where(lower, jnp.exp(spread), 0.0)
    return gamma_row, gamma_end, mask, rate_col


def compose(first, second):
    decay1, m1, b1 = first
    decay2, m2, b2 = second
    both = nn(m1.astype(BF16), jnp.concatenate([m2, b2], axis=1).astype(BF16))
    return decay1 * decay2, decay2 * m1 + decay1 * m2 - both[:, :K], decay1 * b2 + b1 - both[:, K:]


def apply(first, state):
    decay, m, b = first
    return decay * state + b - nn(m.astype(BF16), state.astype(BF16))


def decay_rows(decay, width):
    high = decay.astype(BF16).astype(F32)
    middle = (decay - high).astype(BF16).astype(F32)
    low = decay - high - middle
    rows = lax.broadcasted_iota(jnp.int32, (PAD, width), 0)
    return jnp.where(rows == 0, high, jnp.where(rows == 1, middle, jnp.where(rows == 2, low, 0.0))).astype(BF16)


def decay_from(block):
    return jnp.sum(block.astype(F32), axis=0, keepdims=True)[:, :1]


def unpack(block):
    return decay_from(block[K:]), block[:K, :K].astype(F32), block[:K, K:].astype(F32)


def pack(ref, decayed):
    decay, m, b = decayed
    ref[:K, :K] = m.astype(BF16)
    ref[:K, K:] = b.astype(BF16)
    ref[K:, :] = decay_rows(decay, ref.shape[1])


def keep(ref, decayed):
    decay, m, b = decayed
    ref[:K, :K] = m
    ref[:K, K:] = b
    ref[K:, :] = jnp.broadcast_to(decay, (8, ref.shape[1]))


def kept(ref):
    return ref[K : K + 1, :1], ref[:K, :K], ref[:K, K:]


def choose(flag, if_set, if_not):
    return tuple(jnp.where(flag, p, q) for p, q in zip(if_set, if_not))


def head_rows(kq_ref, which):
    return kq_ref[:, 16 * which : 16 * which + 16, :].reshape(K, 2 * N)


def local_map_kernel(kq_ref, grad_ref, gate_ref, rate_ref, inv_ref, map_ref, wt_ref, lg_ref):
    key_t = head_rows(kq_ref, 0)
    query_t = head_rows(kq_ref, 1)
    maps = []
    for g in range(2):
        span = slice(g * N, (g + 1) * N)
        rate = rate_ref[:, span]
        gamma, gamma_end, mask, _ = gates_of(gate_ref[:, span], rate)
        kt, qt = key_t[:, span], query_t[:, span]
        into = jnp.exp(gamma)
        scaled = (kt * (rate * into)).astype(BF16)
        wt = nt(scaled, inv_ref[g, 0]).astype(BF16)
        wt_ref[:, span] = wt
        score = (tn(qt, kt) * mask).astype(BF16)
        out_t = (kt * jnp.exp(gamma_end - gamma)).astype(BF16)
        in_t = (qt * into).astype(BF16)
        grad = grad_ref[span, :]
        lg = tn(score, grad)
        lg_ref[span, :] = lg
        offset = nn(in_t, grad) - nn2(wt, lg)
        maps.append((jnp.exp(gamma_end), nt(wt, out_t), offset))
    pack(map_ref, compose(*maps))


def pair_kernel(place_ref, own_ref, other_ref, map_ref):
    upper = place_ref[0] == 1

    def half(ref):
        decay, m, b = unpack(ref[...])
        return decay, m, jnp.where(upper, b[:, HALF:], b[:, :HALF])

    own, other = half(own_ref), half(other_ref)
    pack(map_ref, compose(choose(upper, other, own), choose(upper, own, other)))


def first_round_kernel(place_ref, own_ref, other_ref, map_ref, end_ref):
    upper = place_ref[1] == 1
    own, other = unpack(own_ref[...]), unpack(other_ref[...])
    pack(map_ref, compose(choose(upper, other, own), choose(upper, own, other)))
    nothing = (jnp.ones((1, 1), F32), jnp.zeros((K, K), F32), jnp.zeros((K, HALF), F32))
    keep(end_ref, choose(upper, nothing, other))


def second_round_kernel(place_ref, own_ref, other_ref, end_ref, map_ref, new_end_ref):
    upper = place_ref[2] == 1
    own, other, end = unpack(own_ref[...]), unpack(other_ref[...]), kept(end_ref)
    pack(map_ref, compose(choose(upper, other, own), choose(upper, own, other)))
    keep(new_end_ref, choose(upper, end, compose(end, other)))


def last_round_kernel(place_ref, own_ref, other_ref, end_ref, b_ref, new_end_ref):
    upper = place_ref[3] == 1
    own, other, end = unpack(own_ref[...]), unpack(other_ref[...]), kept(end_ref)
    b_ref[...] = apply(choose(upper, other, own), jnp.where(upper, own[2], other[2])).astype(BF16)
    keep(new_end_ref, choose(upper, end, compose(end, other)))


def state_kernel(b_ref, end_ref, state_ref):
    state_ref[...] = apply(kept(end_ref), b_ref[...].astype(F32))


def ahead_kernel(kq_ref, grad_ref, gate_ref, rate_ref, inv_ref, wt_ref, value_ref, state_ref,
                 gq_ref, nv_ref, ct_ref, sum_ref):
    key_t = head_rows(kq_ref, 0)
    query_t = head_rows(kq_ref, 1)
    total = jnp.zeros((1, 1), F32)
    for g in range(2):
        span = slice(g * N, (g + 1) * N)
        gamma, _, mask, rate_col = gates_of(gate_ref[:, span], rate_ref[:, span])
        kt, qt = key_t[:, span], query_t[:, span]
        state = state_ref[:, g].reshape(K, V)
        grad = grad_ref[span, :]
        scaled = (value_ref[span, :] * rate_col).astype(BF16)
        fresh = (nn(inv_ref[g, 0], scaled) - tn(wt_ref[:, span], state)).astype(BF16)
        nv_ref[span, :] = fresh
        score = (nt(grad, fresh) * mask).astype(BF16)
        gq = (jnp.exp(gamma) * nt(state, grad) + nt(kt, score)).astype(BF16)
        gq_ref[:, :, span] = gq.reshape(16, 16, N)
        ct_ref[:, span] = nn(qt, score)
        total += jnp.sum(jnp.square(gq.astype(F32)), keepdims=True)
    sum_ref[...] = jnp.broadcast_to(total, (8, 128))


def final_kernel(place_ref, half_ref, other_ref, kq_ref, grad_ref, gate_ref, rate_ref, inv_ref, wt_ref, lg_ref,
                 state_ref, nv_ref, ct_ref, sum_ref, gk_ref, gv_ref, total_ref):
    key_t = head_rows(kq_ref, 0)
    query_t = head_rows(kq_ref, 1)
    state_grad = jnp.concatenate([half_ref[0], half_ref[1]], axis=1)
    state_grad = jnp.where(place_ref[0] == 0, apply(unpack(other_ref[...]), state_grad), state_grad)
    total = sum_ref[:1, :1]
    for g in (1, 0):
        span = slice(g * N, (g + 1) * N)
        rate = rate_ref[:, span]
        gamma, gamma_end, _, rate_col = gates_of(gate_ref[:, span], rate)
        into = jnp.exp(gamma)
        away = jnp.exp(gamma_end - gamma)
        inverse = inv_ref[g, 0]
        out_t = (key_t[:, span] * away).astype(BF16)
        high, low = split(state_grad)
        value_grad = lg_ref[span, :] + tn(out_t, high) + tn(out_t, low)
        rounded = value_grad.astype(BF16)
        gv = (rate_col * tn(inverse, rounded)).astype(BF16)
        gv_ref[span, :] = gv
        write_t = (-nt(state_ref[:, g].reshape(K, V), rounded)).astype(BF16)
        gk = (ct_ref[:, span] + away * nt(high, nv_ref[span, :]) + (rate * into) * nn(write_t, inverse)).astype(BF16)
        gk_ref[:, :, span] = gk.reshape(16, 16, N)
        total += jnp.sum(jnp.square(gk.astype(F32)), keepdims=True) + jnp.sum(
            jnp.square(gv.astype(F32)), keepdims=True
        )
        if g == 1:
            in_t = (query_t[:, span] * into).astype(BF16)
            state_grad = (
                jnp.exp(gamma_end) * state_grad
                + nn(in_t, grad_ref[span, :])
                - nn2(wt_ref[:, span], value_grad)
            )
    total_ref[...] = jnp.broadcast_to(total[None], (32, 1, 128))


def join_kernel(key_ref, query_ref, out_ref):
    out_ref[:, :16, :] = key_ref[...]
    out_ref[:, 16:, :] = query_ref[...]


def send_kernel(gq_ref, gk_ref, parts_ref, out_ref):
    total = jnp.sum(parts_ref[...], axis=0)
    high = total.astype(BF16).astype(F32)
    middle = (total - high).astype(BF16).astype(F32)
    low = total - high - middle
    rows = lax.broadcasted_iota(jnp.int32, (16, N), 0)
    pieces = jnp.where(rows == 0, high, jnp.where(rows == 1, middle, jnp.where(rows == 2, low, 0.0)))
    for at, ref in ((0, gq_ref), (32, gk_ref)):
        out_ref[:, at : at + 16, :] = ref[:, :, :N]
        out_ref[:, at + 16 : at + 32, :] = ref[:, :, N:]
    out_ref[:, 64:, :] = jnp.broadcast_to(pieces.astype(BF16)[None], (16, 16, N))


def receive_kernel(back_ref, gq_ref, gk_ref, square_ref):
    for at, ref in ((0, gq_ref), (32, gk_ref)):
        ref[:, :, :N] = back_ref[:, at : at + 16, :]
        ref[:, :, N:] = back_ref[:, at + 16 : at + 32, :]
    pieces = jnp.sum(back_ref[:, 64:, :].astype(F32), axis=0)
    total = jnp.sum(pieces, axis=0, keepdims=True)
    square_ref[...] = total[:, :1] * (1.0 / (8192 * 16 * (2 * K + V)))


def call(kernel, outs, args, flops, scratch=(), scalars=0):
    spec = pl.BlockSpec(memory_space=pltpu.VMEM)
    smem = pl.BlockSpec(memory_space=pltpu.SMEM)
    moved = sum(a.size * a.dtype.itemsize for a in args)
    return pl.pallas_call(
        kernel,
        out_shape=outs,
        in_specs=[smem] * scalars + [spec] * (len(args) - scalars),
        out_specs=[spec] * len(outs),
        scratch_shapes=list(scratch),
        cost_estimate=pl.CostEstimate(flops=flops, bytes_accessed=moved, transcendentals=0),
        compiler_params=pltpu.CompilerParams(vmem_limit_bytes=24 * 2**20),
    )(*args)


def shape(dims, dtype=BF16):
    return jax.ShapeDtypeStruct(dims, dtype)


def to_heads(array):
    return lax.all_to_all(array, "key", 0, 0, tiled=True)


def local(query_rows, key_rows, value_rows, out_grad, log_gates, write_rate, group_inverse, states):
    keys = jnp.transpose(key_rows, (1, 2, 0))
    queries = jnp.transpose(query_rows, (1, 2, 0))
    (joined,) = call(join_kernel, [shape((16, 32, 2 * N))], (keys, queries), 0)
    kq = to_heads(joined)
    grad = out_grad.reshape(2 * N, V)
    values = value_rows.reshape(2 * N, V)
    x, y, c = (lax.axis_index(name) for name in SEQ)
    place = jnp.stack([c, y & 1, y >> 1, x & 1]).astype(jnp.int32)
    chip_map = shape((K + PAD, K + HALF))
    end_map = shape((K + 8, K + HALF), F32)
    square = shape((K, V), F32)
    basics = (kq, grad, log_gates, write_rate, group_inverse)

    device_map, written_t, local_grad = call(
        local_map_kernel, [shape((K + PAD, K + V)), shape((K, 2 * N)), square], basics, 10**8
    )
    states, device_map = lax.optimization_barrier((states, device_map))
    state_heads = to_heads(jnp.transpose(states, (1, 0, 2, 3)))
    chip_other = lax.ppermute(device_map, "c", [(0, 1), (1, 0)])
    (now,) = call(pair_kernel, [chip_map], (place, device_map, chip_other), HIDING, scalars=1)
    other = lax.ppermute(now, "y", PAIRS)
    now, end = call(first_round_kernel, [chip_map, end_map], (place, now, other), 10**8, scalars=1)
    other = lax.ppermute(now, "y", CROSS)
    now, end = call(second_round_kernel, [chip_map, end_map], (place, now, other, end), 10**8, scalars=1)
    other = lax.ppermute(now, "x", PAIRS)
    now, end = call(
        last_round_kernel, [shape((K, HALF)), end_map], (place, now, other, end), 10**8, scalars=1
    )
    later = lax.ppermute(now, "x", [(2, 1), (3, 0)])

    gq, fresh, score_term, query_sum = call(
        ahead_kernel,
        [shape((16, 16, 2 * N)), shape((2 * N, V)), square, shape((8, 128), F32)],
        (*basics, written_t, values, state_heads),
        2 * 10**8,
    )
    later, gq = lax.optimization_barrier((later, gq))
    (state_half,) = call(state_kernel, [shape((K, HALF), F32)], (later, end), 10**8)
    state_halves = lax.all_gather(state_half, "c")
    gk, grad_value, total = call(
        final_kernel,
        [shape((16, 16, 2 * N)), shape((2 * N, V)), shape((32, 1, 128), F32)],
        (place, state_halves, chip_other, *basics, written_t, local_grad, state_heads, fresh, score_term, query_sum),
        4 * 10**8,
        scalars=1,
    )
    parts = lax.all_to_all(total, SEQ, 0, 0, tiled=True)
    (sent,) = call(send_kernel, [shape((16, 80, N))], (gq, gk, parts), 10**6)
    grad_query, grad_key, grad_square = call(
        receive_kernel,
        [shape((16, 16, 2 * N)), shape((16, 16, 2 * N)), shape((1, 1), F32)],
        (to_heads(sent),),
        10**6,
    )
    return (
        jnp.transpose(grad_query, (2, 0, 1)),
        jnp.transpose(grad_key, (2, 0, 1)),
        grad_value.reshape(2 * N, 1, V),
        grad_square.reshape(()),
    )


def solution(mesh):
    grid = Mesh(mesh.devices.reshape(4, 4, 2, 16), ("x", "y", "c", "key"))
    in_specs = (
        P(SEQ, None, "key"),
        P(SEQ, None, "key"),
        P(SEQ, "key", None),
        P(SEQ, "key", None),
        P("key", SEQ),
        P("key", SEQ),
        P(SEQ, "key", None, None),
        P(SEQ, None, "key", None),
    )
    out_specs = (P(SEQ, None, "key"), P(SEQ, None, "key"), P(SEQ, "key", None), P())
    return jax.shard_map(local, mesh=grid, in_specs=in_specs, out_specs=out_specs, check_vma=False)
```

```python
import jax
import jax.numpy as jnp
from jax import lax
from jax.experimental import pallas as pl
from jax.experimental.pallas import tpu as pltpu
from jax.sharding import Mesh, PartitionSpec as P

F32 = jnp.float32
BF16 = jnp.bfloat16
SEQ = ("x", "y", "c")
N = 128
K = 256
V = 256
HALF = V // 2
PAD = 16
HIDING = 6 * 10**10


def nn(a, b):
    return lax.dot_general(a, b, (((1,), (0,)), ((), ())), preferred_element_type=F32)


def nt(a, b):
    return lax.dot_general(a, b, (((1,), (1,)), ((), ())), preferred_element_type=F32)


def tn(a, b):
    return lax.dot_general(a, b, (((0,), (0,)), ((), ())), preferred_element_type=F32)


def split(a):
    high = a.astype(BF16)
    return high, (a - high.astype(F32)).astype(BF16)


def nn2(a, b):
    high, low = split(b)
    return nn(a, high) + nn(a, low)


def tn2(a, b):
    high, low = split(b)
    return tn(a, high) + tn(a, low)


def gates_of(gate_row, rate_row):
    rows = lax.broadcasted_iota(jnp.int32, (N, N), 0)
    cols = lax.broadcasted_iota(jnp.int32, (N, N), 1)
    lower = cols <= rows
    eye = cols == rows
    gate_col = jnp.sum(jnp.where(eye, gate_row, 0.0), axis=1, keepdims=True)
    rate_col = jnp.sum(jnp.where(eye, rate_row, 0.0), axis=1, keepdims=True)
    gamma_col = jnp.sum(jnp.where(lower, gate_row, 0.0), axis=1, keepdims=True)
    gamma_row = jnp.sum(jnp.where(rows <= cols, gate_col, 0.0), axis=0, keepdims=True)
    gamma_end = jnp.sum(gate_row, axis=1, keepdims=True)
    spread = jnp.where(lower, gamma_col - gamma_row, 0.0)
    mask = jnp.where(lower, jnp.exp(spread), 0.0)
    return gamma_row, gamma_end, mask, rate_col


def compose(first, second):
    decay1, m1, b1 = first
    decay2, m2, b2 = second
    both = nn(m1.astype(BF16), jnp.concatenate([m2, b2], axis=1).astype(BF16))
    return decay1 * decay2, decay2 * m1 + decay1 * m2 - both[:, :K], decay1 * b2 + b1 - both[:, K:]


def apply(first, state):
    decay, m, b = first
    return decay * state + b - nn(m.astype(BF16), state.astype(BF16))


def decay_rows(decay, width):
    high = decay.astype(BF16).astype(F32)
    middle = (decay - high).astype(BF16).astype(F32)
    low = decay - high - middle
    rows = lax.broadcasted_iota(jnp.int32, (PAD, width), 0)
    return jnp.where(rows == 0, high, jnp.where(rows == 1, middle, jnp.where(rows == 2, low, 0.0))).astype(BF16)


def decay_from(block):
    return jnp.sum(block.astype(F32), axis=0, keepdims=True)[:, :1]


def unpack(block):
    return decay_from(block[K:]), block[:K, :K].astype(F32), block[:K, K:].astype(F32)


def pack(ref, decayed):
    decay, m, b = decayed
    ref[:K, :K] = m.astype(BF16)
    ref[:K, K:] = b.astype(BF16)
    ref[K:, :] = decay_rows(decay, ref.shape[1])


def keep(ref, decayed):
    decay, m, b = decayed
    ref[:K, :K] = m
    ref[:K, K:] = b
    ref[K:, :] = jnp.broadcast_to(decay, (8, ref.shape[1]))


def kept(ref):
    return ref[K : K + 1, :1], ref[:K, :K], ref[:K, K:]


def choose(flag, if_set, if_not):
    return tuple(jnp.where(flag, p, q) for p, q in zip(if_set, if_not))


def head_rows(kq_ref, which):
    return kq_ref[:, 16 * which : 16 * which + 16, :].reshape(K, 2 * N)


def local_map_kernel(kq_ref, grad_ref, gate_ref, rate_ref, inv_ref, map_ref, wt_ref, lg_ref):
    key_t = head_rows(kq_ref, 0)
    query_t = head_rows(kq_ref, 1)
    maps = []
    for g in range(2):
        span = slice(g * N, (g + 1) * N)
        rate = rate_ref[:, span]
        gamma, gamma_end, mask, _ = gates_of(gate_ref[:, span], rate)
        kt, qt = key_t[:, span], query_t[:, span]
        into = jnp.exp(gamma)
        scaled = (kt * (rate * into)).astype(BF16)
        wt = nt(scaled, inv_ref[g, 0]).astype(BF16)
        wt_ref[:, span] = wt
        score = (tn(qt, kt) * mask).astype(BF16)
        out_t = (kt * jnp.exp(gamma_end - gamma)).astype(BF16)
        in_t = (qt * into).astype(BF16)
        grad = grad_ref[span, :]
        lg = tn(score, grad)
        lg_ref[span, :] = lg
        offset = nn(in_t, grad) - nn2(wt, lg)
        maps.append((jnp.exp(gamma_end), nt(wt, out_t), offset))
    pack(map_ref, compose(*maps))


def pair_kernel(place_ref, own_ref, other_ref, map_ref):
    upper = place_ref[0] == 1

    def half(ref):
        decay, m, b = unpack(ref[...])
        return decay, m, jnp.where(upper, b[:, HALF:], b[:, :HALF])

    own, other = half(own_ref), half(other_ref)
    pack(map_ref, compose(choose(upper, other, own), choose(upper, own, other)))


def plane_kernel(place_ref, chips_ref, map_ref, end_ref):
    suffix = unpack(chips_ref[3])
    end = (jnp.ones((1, 1), F32), jnp.zeros((K, K), F32), jnp.zeros((K, HALF), F32))
    for j in (2, 1, 0):
        end = choose(place_ref[1] == j, suffix, end)
        suffix = compose(unpack(chips_ref[j]), suffix)
    pack(map_ref, suffix)
    keep(end_ref, end)


def state_kernel(place_ref, planes_ref, end_ref, state_ref):
    state = jnp.zeros((K, HALF), F32)
    for j in (3, 2, 1):
        state = jnp.where(place_ref[2] < j, apply(unpack(planes_ref[j]), state), state)
    state_ref[...] = apply(kept(end_ref), state)


def ahead_kernel(kq_ref, grad_ref, gate_ref, rate_ref, inv_ref, wt_ref, value_ref, state_ref,
                 gq_ref, nv_ref, ct_ref, sum_ref):
    key_t = head_rows(kq_ref, 0)
    query_t = head_rows(kq_ref, 1)
    total = jnp.zeros((1, 1), F32)
    for g in range(2):
        span = slice(g * N, (g + 1) * N)
        gamma, _, mask, rate_col = gates_of(gate_ref[:, span], rate_ref[:, span])
        kt, qt = key_t[:, span], query_t[:, span]
        state = state_ref[:, g].reshape(K, V)
        grad = grad_ref[span, :]
        scaled = (value_ref[span, :] * rate_col).astype(BF16)
        fresh = (nn(inv_ref[g, 0], scaled) - tn(wt_ref[:, span], state)).astype(BF16)
        nv_ref[span, :] = fresh
        score = (nt(grad, fresh) * mask).astype(BF16)
        gq = (jnp.exp(gamma) * nt(state, grad) + nt(kt, score)).astype(BF16)
        gq_ref[:, :, span] = gq.reshape(16, 16, N)
        ct_ref[:, span] = nn(qt, score)
        total += jnp.sum(jnp.square(gq.astype(F32)), keepdims=True)
    sum_ref[...] = jnp.broadcast_to(total, (8, 128))


def final_kernel(place_ref, half_ref, other_ref, kq_ref, grad_ref, gate_ref, rate_ref, inv_ref, wt_ref, lg_ref,
                 state_ref, nv_ref, ct_ref, sum_ref, gk_ref, gv_ref, total_ref):
    key_t = head_rows(kq_ref, 0)
    query_t = head_rows(kq_ref, 1)
    state_grad = jnp.concatenate([half_ref[0], half_ref[1]], axis=1)
    state_grad = jnp.where(place_ref[0] == 0, apply(unpack(other_ref[...]), state_grad), state_grad)
    total = sum_ref[:1, :1]
    for g in (1, 0):
        span = slice(g * N, (g + 1) * N)
        rate = rate_ref[:, span]
        gamma, gamma_end, _, rate_col = gates_of(gate_ref[:, span], rate)
        into = jnp.exp(gamma)
        away = jnp.exp(gamma_end - gamma)
        inverse = inv_ref[g, 0]
        out_t = (key_t[:, span] * away).astype(BF16)
        high, low = split(state_grad)
        value_grad = lg_ref[span, :] + tn(out_t, high) + tn(out_t, low)
        rounded = value_grad.astype(BF16)
        gv = (rate_col * tn(inverse, rounded)).astype(BF16)
        gv_ref[span, :] = gv
        write_t = (-nt(state_ref[:, g].reshape(K, V), rounded)).astype(BF16)
        gk = (ct_ref[:, span] + away * nt(high, nv_ref[span, :]) + (rate * into) * nn(write_t, inverse)).astype(BF16)
        gk_ref[:, :, span] = gk.reshape(16, 16, N)
        total += jnp.sum(jnp.square(gk.astype(F32)), keepdims=True) + jnp.sum(
            jnp.square(gv.astype(F32)), keepdims=True
        )
        if g == 1:
            in_t = (query_t[:, span] * into).astype(BF16)
            state_grad = (
                jnp.exp(gamma_end) * state_grad
                + nn(in_t, grad_ref[span, :])
                - nn2(wt_ref[:, span], value_grad)
            )
    total_ref[...] = jnp.broadcast_to(total[None], (32, 1, 128))


def join_kernel(key_ref, query_ref, out_ref):
    out_ref[:, :16, :] = key_ref[...]
    out_ref[:, 16:, :] = query_ref[...]


def send_kernel(gq_ref, gk_ref, parts_ref, out_ref):
    total = jnp.sum(parts_ref[...], axis=0)
    high = total.astype(BF16).astype(F32)
    middle = (total - high).astype(BF16).astype(F32)
    low = total - high - middle
    rows = lax.broadcasted_iota(jnp.int32, (16, N), 0)
    pieces = jnp.where(rows == 0, high, jnp.where(rows == 1, middle, jnp.where(rows == 2, low, 0.0)))
    for at, ref in ((0, gq_ref), (32, gk_ref)):
        out_ref[:, at : at + 16, :] = ref[:, :, :N]
        out_ref[:, at + 16 : at + 32, :] = ref[:, :, N:]
    out_ref[:, 64:, :] = jnp.broadcast_to(pieces.astype(BF16)[None], (16, 16, N))


def receive_kernel(back_ref, gq_ref, gk_ref, square_ref):
    for at, ref in ((0, gq_ref), (32, gk_ref)):
        ref[:, :, :N] = back_ref[:, at : at + 16, :]
        ref[:, :, N:] = back_ref[:, at + 16 : at + 32, :]
    pieces = jnp.sum(back_ref[:, 64:, :].astype(F32), axis=0)
    total = jnp.sum(pieces, axis=0, keepdims=True)
    square_ref[...] = total[:, :1] * (1.0 / (8192 * 16 * (2 * K + V)))


def call(kernel, outs, args, flops, scratch=(), scalars=0):
    spec = pl.BlockSpec(memory_space=pltpu.VMEM)
    smem = pl.BlockSpec(memory_space=pltpu.SMEM)
    moved = sum(a.size * a.dtype.itemsize for a in args)
    return pl.pallas_call(
        kernel,
        out_shape=outs,
        in_specs=[smem] * scalars + [spec] * (len(args) - scalars),
        out_specs=[spec] * len(outs),
        scratch_shapes=list(scratch),
        cost_estimate=pl.CostEstimate(flops=flops, bytes_accessed=moved, transcendentals=0),
        compiler_params=pltpu.CompilerParams(vmem_limit_bytes=24 * 2**20),
    )(*args)


def shape(dims, dtype=BF16):
    return jax.ShapeDtypeStruct(dims, dtype)


def to_heads(array):
    return lax.all_to_all(array, "key", 0, 0, tiled=True)


def local(query_rows, key_rows, value_rows, out_grad, log_gates, write_rate, group_inverse, states):
    keys = jnp.transpose(key_rows, (1, 2, 0))
    queries = jnp.transpose(query_rows, (1, 2, 0))
    (joined,) = call(join_kernel, [shape((16, 32, 2 * N))], (keys, queries), 0)
    kq = to_heads(joined)
    grad = out_grad.reshape(2 * N, V)
    values = value_rows.reshape(2 * N, V)
    x, y, c = (lax.axis_index(name) for name in SEQ)
    place = jnp.stack([c, y, x]).astype(jnp.int32)
    chip_map = shape((K + PAD, K + HALF))
    end_map = shape((K + 8, K + HALF), F32)
    square = shape((K, V), F32)
    basics = (kq, grad, log_gates, write_rate, group_inverse)

    device_map, written_t, local_grad = call(
        local_map_kernel, [shape((K + PAD, K + V)), shape((K, 2 * N)), square], basics, 10**8
    )
    states, device_map = lax.optimization_barrier((states, device_map))
    state_heads = to_heads(jnp.transpose(states, (1, 0, 2, 3)))
    chip_other = lax.ppermute(device_map, "c", [(0, 1), (1, 0)])
    (now,) = call(pair_kernel, [chip_map], (place, device_map, chip_other), HIDING, scalars=1)
    now, end = call(plane_kernel, [chip_map, end_map], (place, lax.all_gather(now, "y")), 10**8, scalars=1)
    planes = lax.all_gather(now, "x")

    gq, fresh, score_term, query_sum = call(
        ahead_kernel,
        [shape((16, 16, 2 * N)), shape((2 * N, V)), square, shape((8, 128), F32)],
        (*basics, written_t, values, state_heads),
        2 * 10**8,
    )
    (state_half,) = call(state_kernel, [shape((K, HALF), F32)], (place, planes, end), 10**8, scalars=1)
    state_halves = lax.all_gather(state_half, "c")
    gk, grad_value, total = call(
        final_kernel,
        [shape((16, 16, 2 * N)), shape((2 * N, V)), shape((32, 1, 128), F32)],
        (place, state_halves, chip_other, *basics, written_t, local_grad, state_heads, fresh, score_term, query_sum),
        4 * 10**8,
        scalars=1,
    )
    parts = lax.all_to_all(total, SEQ, 0, 0, tiled=True)
    (sent,) = call(send_kernel, [shape((16, 80, N))], (gq, gk, parts), 10**6)
    grad_query, grad_key, grad_square = call(
        receive_kernel,
        [shape((16, 16, 2 * N)), shape((16, 16, 2 * N)), shape((1, 1), F32)],
        (to_heads(sent),),
        10**6,
    )
    return (
        jnp.transpose(grad_query, (2, 0, 1)),
        jnp.transpose(grad_key, (2, 0, 1)),
        grad_value.reshape(2 * N, 1, V),
        grad_square.reshape(()),
    )


def solution(mesh):
    grid = Mesh(mesh.devices.reshape(4, 4, 2, 16), ("x", "y", "c", "key"))
    in_specs = (
        P(SEQ, None, "key"),
        P(SEQ, None, "key"),
        P(SEQ, "key", None),
        P(SEQ, "key", None),
        P("key", SEQ),
        P("key", SEQ),
        P(SEQ, "key", None, None),
        P(SEQ, None, "key", None),
    )
    out_specs = (P(SEQ, None, "key"), P(SEQ, None, "key"), P(SEQ, "key", None), P())
    return jax.shard_map(local, mesh=grid, in_specs=in_specs, out_specs=out_specs, check_vma=False)
```

```python
import jax
import jax.numpy as jnp
from jax import lax
from jax.experimental import pallas as pl
from jax.experimental.pallas import tpu as pltpu
from jax.sharding import Mesh, PartitionSpec as P

F32 = jnp.float32
BF16 = jnp.bfloat16
SEQ = ("x", "y", "c")
N = 128
K = 256
V = 256
HALF = V // 2
PAD = 16
ROWS = K + PAD
HIDING = 6 * 10**10


def nn(a, b):
    return lax.dot_general(a, b, (((1,), (0,)), ((), ())), preferred_element_type=F32)


def nt(a, b):
    return lax.dot_general(a, b, (((1,), (1,)), ((), ())), preferred_element_type=F32)


def tn(a, b):
    return lax.dot_general(a, b, (((0,), (0,)), ((), ())), preferred_element_type=F32)


def split(a):
    high = a.astype(BF16)
    return high, (a - high.astype(F32)).astype(BF16)


def nn2(a, b):
    high, low = split(b)
    return nn(a, high) + nn(a, low)


def tn2(a, b):
    high, low = split(b)
    return tn(a, high) + tn(a, low)


def gates_of(gate_row, rate_row):
    rows = lax.broadcasted_iota(jnp.int32, (N, N), 0)
    cols = lax.broadcasted_iota(jnp.int32, (N, N), 1)
    lower = cols <= rows
    eye = cols == rows
    gate_col = jnp.sum(jnp.where(eye, gate_row, 0.0), axis=1, keepdims=True)
    rate_col = jnp.sum(jnp.where(eye, rate_row, 0.0), axis=1, keepdims=True)
    gamma_col = jnp.sum(jnp.where(lower, gate_row, 0.0), axis=1, keepdims=True)
    gamma_row = jnp.sum(jnp.where(rows <= cols, gate_col, 0.0), axis=0, keepdims=True)
    gamma_end = jnp.sum(gate_row, axis=1, keepdims=True)
    spread = jnp.where(lower, gamma_col - gamma_row, 0.0)
    mask = jnp.where(lower, jnp.exp(spread), 0.0)
    return gamma_row, gamma_end, mask, rate_col


def compose(first, second):
    decay1, m1, b1 = first
    decay2, m2, b2 = second
    both = nn(m1.astype(BF16), jnp.concatenate([m2, b2], axis=1).astype(BF16))
    return decay1 * decay2, decay2 * m1 + decay1 * m2 - both[:, :K], decay1 * b2 + b1 - both[:, K:]


def apply(first, state):
    decay, m, b = first
    return decay * state + b - nn(m.astype(BF16), state.astype(BF16))


def decay_rows(decay, width):
    high = decay.astype(BF16).astype(F32)
    middle = (decay - high).astype(BF16).astype(F32)
    low = decay - high - middle
    rows = lax.broadcasted_iota(jnp.int32, (PAD, width), 0)
    return jnp.where(rows == 0, high, jnp.where(rows == 1, middle, jnp.where(rows == 2, low, 0.0))).astype(BF16)


def decay_from(block):
    return jnp.sum(block.astype(F32), axis=0, keepdims=True)[:, :1]


def unpack(block):
    return decay_from(block[K:]), block[:K, :K].astype(F32), block[:K, K:].astype(F32)


def pack(ref, decayed):
    decay, m, b = decayed
    ref[:K, :K] = m.astype(BF16)
    ref[:K, K:] = b.astype(BF16)
    ref[K:, :] = decay_rows(decay, ref.shape[1])


def choose(flag, if_set, if_not):
    return tuple(jnp.where(flag, p, q) for p, q in zip(if_set, if_not))


def head_rows(kq_ref, which):
    return kq_ref[:, 16 * which : 16 * which + 16, :].reshape(K, 2 * N)


def local_map_kernel(kq_ref, grad_ref, gate_ref, rate_ref, inv_ref, map_ref, wt_ref, lg_ref):
    key_t = head_rows(kq_ref, 0)
    query_t = head_rows(kq_ref, 1)
    maps = []
    for g in range(2):
        span = slice(g * N, (g + 1) * N)
        rate = rate_ref[:, span]
        gamma, gamma_end, mask, _ = gates_of(gate_ref[:, span], rate)
        kt, qt = key_t[:, span], query_t[:, span]
        into = jnp.exp(gamma)
        scaled = (kt * (rate * into)).astype(BF16)
        wt = nt(scaled, inv_ref[g, 0]).astype(BF16)
        wt_ref[:, span] = wt
        score = (tn(qt, kt) * mask).astype(BF16)
        out_t = (kt * jnp.exp(gamma_end - gamma)).astype(BF16)
        in_t = (qt * into).astype(BF16)
        grad = grad_ref[span, :]
        lg = tn(score, grad)
        lg_ref[span, :] = lg
        offset = nn(in_t, grad) - nn2(wt, lg)
        maps.append((jnp.exp(gamma_end), nt(wt, out_t), offset))
    pack(map_ref, compose(*maps))


def pair_kernel(place_ref, own_ref, other_ref, map_ref):
    upper = place_ref[0] == 1

    def half(ref):
        decay, m, b = unpack(ref[...])
        return decay, m, jnp.where(upper, b[:, HALF:], b[:, :HALF])

    own, other = half(own_ref), half(other_ref)
    pack(map_ref, compose(choose(upper, other, own), choose(upper, own, other)))


def plane_kernel(place_ref, chips_ref, send_ref, end_ref, end_b_ref):
    suffix = unpack(chips_ref[3])
    end = (jnp.ones((1, 1), F32), jnp.zeros((K, K), F32), jnp.zeros((K, HALF), F32))
    for j in (2, 1, 0):
        end = choose(place_ref[1] == j, suffix, end)
        suffix = compose(unpack(chips_ref[j]), suffix)
    decay, m, b = suffix
    m_half = jnp.where(place_ref[0] == 0, m[:, :HALF], m[:, HALF:])
    send_ref[:K, :HALF] = m_half.astype(BF16)
    send_ref[:K, HALF:] = b.astype(BF16)
    send_ref[K:, :] = decay_rows(decay, 2 * HALF)
    decay, m, b = end
    end_ref[:K, :] = m
    end_ref[K:, :] = jnp.broadcast_to(decay, (8, K))
    end_b_ref[...] = b.astype(BF16)


def ahead_kernel(kq_ref, grad_ref, gate_ref, rate_ref, inv_ref, wt_ref, value_ref, state_ref,
                 gq_ref, nv_ref, ct_ref, sum_ref):
    key_t = head_rows(kq_ref, 0)
    query_t = head_rows(kq_ref, 1)
    total = jnp.zeros((1, 1), F32)
    for g in range(2):
        span = slice(g * N, (g + 1) * N)
        gamma, _, mask, rate_col = gates_of(gate_ref[:, span], rate_ref[:, span])
        kt, qt = key_t[:, span], query_t[:, span]
        state = state_ref[:, g].reshape(K, V)
        grad = grad_ref[span, :]
        scaled = (value_ref[span, :] * rate_col).astype(BF16)
        fresh = (nn(inv_ref[g, 0], scaled) - tn(wt_ref[:, span], state)).astype(BF16)
        nv_ref[span, :] = fresh
        score = (nt(grad, fresh) * mask).astype(BF16)
        gq = (jnp.exp(gamma) * nt(state, grad) + nt(kt, score)).astype(BF16)
        gq_ref[:, :, span] = gq.reshape(16, 16, N)
        ct_ref[:, span] = nn(qt, score)
        total += jnp.sum(jnp.square(gq.astype(F32)), keepdims=True)
    sum_ref[...] = jnp.broadcast_to(total, (8, 128))


def state_after(place_ref, halves_ref, end_ref, other_ref):
    low, high = (halves_ref[i, 2 * ROWS :, :].astype(F32) for i in range(2))
    state = jnp.concatenate([low[:, :HALF], high[:, :HALF]], axis=1)
    end_b = jnp.concatenate([low[:, HALF:], high[:, HALF:]], axis=1)
    for d in (1, 0):
        low, high = (halves_ref[i, ROWS * d : ROWS * (d + 1), :] for i in range(2))
        m = jnp.concatenate([low[:K, :HALF], high[:K, :HALF]], axis=1)
        b = jnp.concatenate([low[:K, HALF:], high[:K, HALF:]], axis=1).astype(F32)
        state = apply((decay_from(low[K:]), m, b), state)
    state = apply((end_ref[K : K + 1, :1], end_ref[:K, :], end_b), state)
    return jnp.where(place_ref[0] == 0, apply(unpack(other_ref[...]), state), state)


def final_kernel(place_ref, halves_ref, end_ref, other_ref, kq_ref, grad_ref, gate_ref, rate_ref, inv_ref, wt_ref,
                 lg_ref, state_ref, nv_ref, ct_ref, sum_ref, gk_ref, gv_ref, total_ref):
    key_t = head_rows(kq_ref, 0)
    query_t = head_rows(kq_ref, 1)
    state_grad = state_after(place_ref, halves_ref, end_ref, other_ref)
    total = sum_ref[:1, :1]
    for g in (1, 0):
        span = slice(g * N, (g + 1) * N)
        rate = rate_ref[:, span]
        gamma, gamma_end, _, rate_col = gates_of(gate_ref[:, span], rate)
        into = jnp.exp(gamma)
        away = jnp.exp(gamma_end - gamma)
        inverse = inv_ref[g, 0]
        out_t = (key_t[:, span] * away).astype(BF16)
        high, low = split(state_grad)
        value_grad = lg_ref[span, :] + tn(out_t, high) + tn(out_t, low)
        rounded = value_grad.astype(BF16)
        gv = (rate_col * tn(inverse, rounded)).astype(BF16)
        gv_ref[span, :] = gv
        write_t = (-nt(state_ref[:, g].reshape(K, V), rounded)).astype(BF16)
        gk = (ct_ref[:, span] + away * nt(high, nv_ref[span, :]) + (rate * into) * nn(write_t, inverse)).astype(BF16)
        gk_ref[:, :, span] = gk.reshape(16, 16, N)
        total += jnp.sum(jnp.square(gk.astype(F32)), keepdims=True) + jnp.sum(
            jnp.square(gv.astype(F32)), keepdims=True
        )
        if g == 1:
            in_t = (query_t[:, span] * into).astype(BF16)
            state_grad = (
                jnp.exp(gamma_end) * state_grad
                + nn(in_t, grad_ref[span, :])
                - nn2(wt_ref[:, span], value_grad)
            )
    total_ref[...] = jnp.broadcast_to(total, (8, 128))


def join_kernel(key_ref, query_ref, out_ref):
    out_ref[:, :16, :] = key_ref[...]
    out_ref[:, 16:, :] = query_ref[...]


def send_kernel(gk_ref, total_ref, out_ref):
    total = total_ref[:1, :]
    high = total.astype(BF16).astype(F32)
    middle = (total - high).astype(BF16).astype(F32)
    low = total - high - middle
    rows = lax.broadcasted_iota(jnp.int32, (16, N), 0)
    pieces = jnp.where(rows == 0, high, jnp.where(rows == 1, middle, jnp.where(rows == 2, low, 0.0)))
    out_ref[:, :16, :] = gk_ref[:, :, :N]
    out_ref[:, 16:32, :] = gk_ref[:, :, N:]
    out_ref[:, 32:, :] = jnp.broadcast_to(pieces.astype(BF16)[None], (16, 16, N))


def receive_kernel(back_ref, gk_ref, square_ref):
    gk_ref[:, :, :N] = back_ref[:, :16, :]
    gk_ref[:, :, N:] = back_ref[:, 16:32, :]
    pieces = jnp.sum(back_ref[:, 32:, :].astype(F32), axis=0)
    total = jnp.sum(pieces, axis=0, keepdims=True)
    square_ref[...] = total[:, :1] * (1.0 / (8192 * 16 * (2 * K + V)))


def call(kernel, outs, args, flops, scratch=(), scalars=0):
    spec = pl.BlockSpec(memory_space=pltpu.VMEM)
    smem = pl.BlockSpec(memory_space=pltpu.SMEM)
    moved = sum(a.size * a.dtype.itemsize for a in args)
    return pl.pallas_call(
        kernel,
        out_shape=outs,
        in_specs=[smem] * scalars + [spec] * (len(args) - scalars),
        out_specs=[spec] * len(outs),
        scratch_shapes=list(scratch),
        cost_estimate=pl.CostEstimate(flops=flops, bytes_accessed=moved, transcendentals=0),
        compiler_params=pltpu.CompilerParams(vmem_limit_bytes=24 * 2**20),
    )(*args)


def shape(dims, dtype=BF16):
    return jax.ShapeDtypeStruct(dims, dtype)


def to_heads(array):
    return lax.all_to_all(array, "key", 0, 0, tiled=True)


def local(query_rows, key_rows, value_rows, out_grad, log_gates, write_rate, group_inverse, states):
    keys = jnp.transpose(key_rows, (1, 2, 0))
    queries = jnp.transpose(query_rows, (1, 2, 0))
    (joined,) = call(join_kernel, [shape((16, 32, 2 * N))], (keys, queries), 0)
    kq = to_heads(joined)
    grad = out_grad.reshape(2 * N, V)
    values = value_rows.reshape(2 * N, V)
    x, y, c = (lax.axis_index(name) for name in SEQ)
    place = jnp.stack([c, y, x]).astype(jnp.int32)
    chip_map = shape((K + PAD, K + HALF))
    square = shape((K, V), F32)
    basics = (kq, grad, log_gates, write_rate, group_inverse)

    device_map, written_t, local_grad = call(
        local_map_kernel, [shape((K + PAD, K + V)), shape((K, 2 * N)), square], basics, 10**8
    )
    states, device_map = lax.optimization_barrier((states, device_map))
    state_heads = to_heads(jnp.transpose(states, (1, 0, 2, 3)))
    chip_other = lax.ppermute(device_map, "c", [(0, 1), (1, 0)])
    (now,) = call(pair_kernel, [chip_map], (place, device_map, chip_other), HIDING, scalars=1)
    plane_half, end, end_b = call(
        plane_kernel,
        [shape((ROWS, 2 * HALF)), shape((K + 8, K), F32), shape((K, HALF))],
        (place, lax.all_gather(now, "y")),
        10**8,
        scalars=1,
    )
    later = [lax.ppermute(plane_half, "x", [(s, s - d) for s in range(d, 4)]) for d in (1, 2, 3)]

    gq, fresh, score_term, query_sum = call(
        ahead_kernel,
        [shape((16, 16, 2 * N)), shape((2 * N, V)), square, shape((8, 128), F32)],
        (*basics, written_t, values, state_heads),
        2 * 10**8,
    )
    grad_query = to_heads(gq)
    later, fresh = lax.optimization_barrier((later, fresh))
    last = jnp.concatenate([later[2][:K, HALF:], end_b], axis=1)
    halves = lax.all_gather(jnp.concatenate([later[0], later[1], last], axis=0), "c")
    gk, grad_value, total = call(
        final_kernel,
        [shape((16, 16, 2 * N)), shape((2 * N, V)), shape((8, 128), F32)],
        (
            place, halves, end, chip_other, *basics, written_t, local_grad, state_heads, fresh, score_term,
            query_sum,
        ),
        4 * 10**8,
        scalars=1,
    )
    for axis in ("c", "y", "x"):
        total = lax.optimization_barrier(lax.psum(total, axis))
    (sent,) = call(send_kernel, [shape((16, 48, N))], (gk, total), 10**6)
    grad_key, grad_square = call(
        receive_kernel, [shape((16, 16, 2 * N)), shape((1, 1), F32)], (to_heads(sent),), 10**6
    )
    return (
        jnp.transpose(grad_query, (2, 0, 1)),
        jnp.transpose(grad_key, (2, 0, 1)),
        grad_value.reshape(2 * N, 1, V),
        grad_square.reshape(()),
    )


def solution(mesh):
    grid = Mesh(mesh.devices.reshape(4, 4, 2, 16), ("x", "y", "c", "key"))
    in_specs = (
        P(SEQ, None, "key"),
        P(SEQ, None, "key"),
        P(SEQ, "key", None),
        P(SEQ, "key", None),
        P("key", SEQ),
        P("key", SEQ),
        P(SEQ, "key", None, None),
        P(SEQ, None, "key", None),
    )
    out_specs = (P(SEQ, None, "key"), P(SEQ, None, "key"), P(SEQ, "key", None), P())
    return jax.shard_map(local, mesh=grid, in_specs=in_specs, out_specs=out_specs, check_vma=False)
```

```python
import jax
import jax.numpy as jnp
from jax import lax
from jax.experimental import pallas as pl
from jax.experimental.pallas import tpu as pltpu
from jax.sharding import Mesh, PartitionSpec as P

F32 = jnp.float32
BF16 = jnp.bfloat16
SEQ = ("x", "y", "c")
N = 128
K = 256
V = 256
HALF = V // 2
PAD = 16
ROWS = K + PAD
HIDING = 6 * 10**10


def nn(a, b):
    return lax.dot_general(a, b, (((1,), (0,)), ((), ())), preferred_element_type=F32)


def nt(a, b):
    return lax.dot_general(a, b, (((1,), (1,)), ((), ())), preferred_element_type=F32)


def tn(a, b):
    return lax.dot_general(a, b, (((0,), (0,)), ((), ())), preferred_element_type=F32)


def split(a):
    high = a.astype(BF16)
    return high, (a - high.astype(F32)).astype(BF16)


def nn2(a, b):
    high, low = split(b)
    return nn(a, high) + nn(a, low)


def tn2(a, b):
    high, low = split(b)
    return tn(a, high) + tn(a, low)


def gates_of(gate_row, rate_row):
    rows = lax.broadcasted_iota(jnp.int32, (N, N), 0)
    cols = lax.broadcasted_iota(jnp.int32, (N, N), 1)
    lower = cols <= rows
    eye = cols == rows
    gate_col = jnp.sum(jnp.where(eye, gate_row, 0.0), axis=1, keepdims=True)
    rate_col = jnp.sum(jnp.where(eye, rate_row, 0.0), axis=1, keepdims=True)
    gamma_col = jnp.sum(jnp.where(lower, gate_row, 0.0), axis=1, keepdims=True)
    gamma_row = jnp.sum(jnp.where(rows <= cols, gate_col, 0.0), axis=0, keepdims=True)
    gamma_end = jnp.sum(gate_row, axis=1, keepdims=True)
    spread = jnp.where(lower, gamma_col - gamma_row, 0.0)
    mask = jnp.where(lower, jnp.exp(spread), 0.0)
    return gamma_row, gamma_end, mask, rate_col


def compose(first, second):
    decay1, m1, b1 = first
    decay2, m2, b2 = second
    both = nn(m1.astype(BF16), jnp.concatenate([m2, b2], axis=1).astype(BF16))
    return decay1 * decay2, decay2 * m1 + decay1 * m2 - both[:, :K], decay1 * b2 + b1 - both[:, K:]


def apply(first, state):
    decay, m, b = first
    return decay * state + b - nn(m.astype(BF16), state.astype(BF16))


def decay_rows(decay, width):
    high = decay.astype(BF16).astype(F32)
    middle = (decay - high).astype(BF16).astype(F32)
    low = decay - high - middle
    rows = lax.broadcasted_iota(jnp.int32, (PAD, width), 0)
    return jnp.where(rows == 0, high, jnp.where(rows == 1, middle, jnp.where(rows == 2, low, 0.0))).astype(BF16)


def decay_from(block):
    return jnp.sum(block.astype(F32), axis=0, keepdims=True)[:, :1]


def unpack(block):
    return decay_from(block[K:]), block[:K, :K].astype(F32), block[:K, K:].astype(F32)


def pack(ref, decayed):
    decay, m, b = decayed
    ref[:K, :K] = m.astype(BF16)
    ref[:K, K:] = b.astype(BF16)
    ref[K:, :] = decay_rows(decay, ref.shape[1])


def choose(flag, if_set, if_not):
    return tuple(jnp.where(flag, p, q) for p, q in zip(if_set, if_not))


def head_rows(kq_ref, which):
    return kq_ref[:, 16 * which : 16 * which + 16, :].reshape(K, 2 * N)


def local_map_kernel(kq_ref, grad_ref, gate_ref, rate_ref, inv_ref, map_ref, wt_ref, lg_ref):
    key_t = head_rows(kq_ref, 0)
    query_t = head_rows(kq_ref, 1)
    maps = []
    for g in range(2):
        span = slice(g * N, (g + 1) * N)
        rate = rate_ref[:, span]
        gamma, gamma_end, mask, _ = gates_of(gate_ref[:, span], rate)
        kt, qt = key_t[:, span], query_t[:, span]
        into = jnp.exp(gamma)
        scaled = (kt * (rate * into)).astype(BF16)
        wt = nt(scaled, inv_ref[g, 0]).astype(BF16)
        wt_ref[:, span] = wt
        score = (tn(qt, kt) * mask).astype(BF16)
        out_t = (kt * jnp.exp(gamma_end - gamma)).astype(BF16)
        in_t = (qt * into).astype(BF16)
        grad = grad_ref[span, :]
        lg = tn(score, grad)
        lg_ref[span, :] = lg
        offset = nn(in_t, grad) - nn2(wt, lg)
        maps.append((jnp.exp(gamma_end), nt(wt, out_t), offset))
    pack(map_ref, compose(*maps))


def pair_kernel(place_ref, own_ref, other_ref, map_ref):
    upper = place_ref[0] == 1

    def half(ref):
        decay, m, b = unpack(ref[...])
        return decay, m, jnp.where(upper, b[:, HALF:], b[:, :HALF])

    own, other = half(own_ref), half(other_ref)
    pack(map_ref, compose(choose(upper, other, own), choose(upper, own, other)))


def plane_kernel(place_ref, chips_ref, send_ref, end_ref, end_b_ref):
    suffix = unpack(chips_ref[3])
    end = (jnp.ones((1, 1), F32), jnp.zeros((K, K), F32), jnp.zeros((K, HALF), F32))
    for j in (2, 1, 0):
        end = choose(place_ref[1] == j, suffix, end)
        suffix = compose(unpack(chips_ref[j]), suffix)
    decay, m, b = suffix
    m_half = jnp.where(place_ref[0] == 0, m[:, :HALF], m[:, HALF:])
    send_ref[:K, :HALF] = m_half.astype(BF16)
    send_ref[:K, HALF:] = b.astype(BF16)
    send_ref[K:, :] = decay_rows(decay, 2 * HALF)
    decay, m, b = end
    end_ref[:K, :] = m
    end_ref[K:, :] = jnp.broadcast_to(decay, (8, K))
    end_b_ref[...] = b.astype(BF16)


def ahead_kernel(kq_ref, grad_ref, gate_ref, rate_ref, inv_ref, wt_ref, value_ref, state_ref,
                 gq_ref, nv_ref, ct_ref, sum_ref):
    key_t = head_rows(kq_ref, 0)
    query_t = head_rows(kq_ref, 1)
    total = jnp.zeros((1, 1), F32)
    for g in range(2):
        span = slice(g * N, (g + 1) * N)
        gamma, _, mask, rate_col = gates_of(gate_ref[:, span], rate_ref[:, span])
        kt, qt = key_t[:, span], query_t[:, span]
        state = state_ref[:, g].reshape(K, V)
        grad = grad_ref[span, :]
        scaled = (value_ref[span, :] * rate_col).astype(BF16)
        fresh = (nn(inv_ref[g, 0], scaled) - tn(wt_ref[:, span], state)).astype(BF16)
        nv_ref[span, :] = fresh
        score = (nt(grad, fresh) * mask).astype(BF16)
        gq = (jnp.exp(gamma) * nt(state, grad) + nt(kt, score)).astype(BF16)
        gq_ref[:, :, span] = gq.reshape(16, 16, N)
        ct_ref[:, span] = nn(qt, score)
        total += jnp.sum(jnp.square(gq.astype(F32)), keepdims=True)
    sum_ref[...] = jnp.broadcast_to(total, (8, 128))


def state_after(place_ref, halves_ref, end_ref, other_ref):
    low, high = (halves_ref[i, 2 * ROWS :, :].astype(F32) for i in range(2))
    state = jnp.concatenate([low[:, :HALF], high[:, :HALF]], axis=1)
    end_b = jnp.concatenate([low[:, HALF:], high[:, HALF:]], axis=1)
    for d in (1, 0):
        low, high = (halves_ref[i, ROWS * d : ROWS * (d + 1), :] for i in range(2))
        m = jnp.concatenate([low[:K, :HALF], high[:K, :HALF]], axis=1)
        b = jnp.concatenate([low[:K, HALF:], high[:K, HALF:]], axis=1).astype(F32)
        state = apply((decay_from(low[K:]), m, b), state)
    state = apply((end_ref[K : K + 1, :1], end_ref[:K, :], end_b), state)
    return jnp.where(place_ref[0] == 0, apply(unpack(other_ref[...]), state), state)


def final_kernel(place_ref, halves_ref, end_ref, other_ref, kq_ref, grad_ref, gate_ref, rate_ref, inv_ref, wt_ref,
                 lg_ref, state_ref, nv_ref, ct_ref, sum_ref, gk_ref, gv_ref, total_ref):
    key_t = head_rows(kq_ref, 0)
    query_t = head_rows(kq_ref, 1)
    state_grad = state_after(place_ref, halves_ref, end_ref, other_ref)
    total = sum_ref[:1, :1]
    for g in (1, 0):
        span = slice(g * N, (g + 1) * N)
        rate = rate_ref[:, span]
        gamma, gamma_end, _, rate_col = gates_of(gate_ref[:, span], rate)
        into = jnp.exp(gamma)
        away = jnp.exp(gamma_end - gamma)
        inverse = inv_ref[g, 0]
        out_t = (key_t[:, span] * away).astype(BF16)
        high, low = split(state_grad)
        value_grad = lg_ref[span, :] + tn(out_t, high) + tn(out_t, low)
        rounded = value_grad.astype(BF16)
        gv = (rate_col * tn(inverse, rounded)).astype(BF16)
        gv_ref[span, :] = gv
        write_t = (-nt(state_ref[:, g].reshape(K, V), rounded)).astype(BF16)
        gk = (ct_ref[:, span] + away * nt(high, nv_ref[span, :]) + (rate * into) * nn(write_t, inverse)).astype(BF16)
        gk_ref[:, :, span] = gk.reshape(16, 16, N)
        total += jnp.sum(jnp.square(gk.astype(F32)), keepdims=True) + jnp.sum(
            jnp.square(gv.astype(F32)), keepdims=True
        )
        if g == 1:
            in_t = (query_t[:, span] * into).astype(BF16)
            state_grad = (
                jnp.exp(gamma_end) * state_grad
                + nn(in_t, grad_ref[span, :])
                - nn2(wt_ref[:, span], value_grad)
            )
    total_ref[...] = jnp.broadcast_to(total[None], (32, 1, 128))


def join_kernel(key_ref, query_ref, out_ref, done):
    copies = [
        pltpu.make_async_copy(ref, out_ref.at[:, pl.ds(16 * i, 16), :], done.at[i])
        for i, ref in enumerate((key_ref, query_ref))
    ]
    for copy in copies:
        copy.start()
    for copy in copies:
        copy.wait()


def join(keys, queries):
    spec = pl.BlockSpec(memory_space=pl.ANY)
    return pl.pallas_call(
        join_kernel,
        out_shape=shape((16, 32, 2 * N)),
        in_specs=[spec, spec],
        out_specs=spec,
        scratch_shapes=[pltpu.SemaphoreType.DMA((2,))],
    )(keys, queries)


def send_kernel(gq_ref, gk_ref, parts_ref, out_ref):
    total = jnp.sum(parts_ref[...], axis=0)
    high = total.astype(BF16).astype(F32)
    middle = (total - high).astype(BF16).astype(F32)
    low = total - high - middle
    rows = lax.broadcasted_iota(jnp.int32, (16, N), 0)
    pieces = jnp.where(rows == 0, high, jnp.where(rows == 1, middle, jnp.where(rows == 2, low, 0.0)))
    for at, ref in ((0, gq_ref), (32, gk_ref)):
        out_ref[:, at : at + 16, :] = ref[:, :, :N]
        out_ref[:, at + 16 : at + 32, :] = ref[:, :, N:]
    out_ref[:, 64:, :] = jnp.broadcast_to(pieces.astype(BF16)[None], (16, 16, N))


def receive_kernel(back_ref, gq_ref, gk_ref, square_ref):
    for at, ref in ((0, gq_ref), (32, gk_ref)):
        ref[:, :, :N] = back_ref[:, at : at + 16, :]
        ref[:, :, N:] = back_ref[:, at + 16 : at + 32, :]
    pieces = jnp.sum(back_ref[:, 64:, :].astype(F32), axis=0)
    total = jnp.sum(pieces, axis=0, keepdims=True)
    square_ref[...] = total[:, :1] * (1.0 / (8192 * 16 * (2 * K + V)))


def call(kernel, outs, args, flops, scratch=(), scalars=0):
    spec = pl.BlockSpec(memory_space=pltpu.VMEM)
    smem = pl.BlockSpec(memory_space=pltpu.SMEM)
    moved = sum(a.size * a.dtype.itemsize for a in args)
    return pl.pallas_call(
        kernel,
        out_shape=outs,
        in_specs=[smem] * scalars + [spec] * (len(args) - scalars),
        out_specs=[spec] * len(outs),
        scratch_shapes=list(scratch),
        cost_estimate=pl.CostEstimate(flops=flops, bytes_accessed=moved, transcendentals=0),
        compiler_params=pltpu.CompilerParams(vmem_limit_bytes=24 * 2**20),
    )(*args)


def shape(dims, dtype=BF16):
    return jax.ShapeDtypeStruct(dims, dtype)


def to_heads(array):
    return lax.all_to_all(array, "key", 0, 0, tiled=True)


def local(query_rows, key_rows, value_rows, out_grad, log_gates, write_rate, group_inverse, states):
    keys = jnp.transpose(key_rows, (1, 2, 0))
    queries = jnp.transpose(query_rows, (1, 2, 0))
    kq = to_heads(join(keys, queries))
    grad = out_grad.reshape(2 * N, V)
    values = value_rows.reshape(2 * N, V)
    x, y, c = (lax.axis_index(name) for name in SEQ)
    place = jnp.stack([c, y, x]).astype(jnp.int32)
    chip_map = shape((K + PAD, K + HALF))
    square = shape((K, V), F32)
    basics = (kq, grad, log_gates, write_rate, group_inverse)

    device_map, written_t, local_grad = call(
        local_map_kernel, [shape((K + PAD, K + V)), shape((K, 2 * N)), square], basics, 10**8
    )
    state_blocks, device_map = lax.optimization_barrier((jnp.transpose(states, (1, 0, 2, 3)), device_map))
    state_heads = to_heads(state_blocks)
    chip_other = lax.ppermute(device_map, "c", [(0, 1), (1, 0)])
    (now,) = call(pair_kernel, [chip_map], (place, device_map, chip_other), HIDING, scalars=1)
    plane_half, end, end_b = call(
        plane_kernel,
        [shape((ROWS, 2 * HALF)), shape((K + 8, K), F32), shape((K, HALF))],
        (place, lax.all_gather(now, "y")),
        10**8,
        scalars=1,
    )
    later = [lax.ppermute(plane_half, "x", [(s, s - d) for s in range(d, 4)]) for d in (1, 2, 3)]

    gq, fresh, score_term, query_sum = call(
        ahead_kernel,
        [shape((16, 16, 2 * N)), shape((2 * N, V)), square, shape((8, 128), F32)],
        (*basics, written_t, values, state_heads),
        2 * 10**8,
    )
    later, fresh = lax.optimization_barrier((later, fresh))
    last = jnp.concatenate([later[2][:K, HALF:], end_b], axis=1)
    halves = lax.all_gather(jnp.concatenate([later[0], later[1], last], axis=0), "c")
    gk, grad_value, total = call(
        final_kernel,
        [shape((16, 16, 2 * N)), shape((2 * N, V)), shape((32, 1, 128), F32)],
        (
            place, halves, end, chip_other, *basics, written_t, local_grad, state_heads, fresh, score_term,
            query_sum,
        ),
        4 * 10**8,
        scalars=1,
    )
    parts = lax.all_to_all(total, SEQ, 0, 0, tiled=True)
    (sent,) = call(send_kernel, [shape((16, 80, N))], (gq, gk, parts), 10**6)
    grad_query, grad_key, grad_square = call(
        receive_kernel,
        [shape((16, 16, 2 * N)), shape((16, 16, 2 * N)), shape((1, 1), F32)],
        (to_heads(sent),),
        10**6,
    )
    return (
        jnp.transpose(grad_query, (2, 0, 1)),
        jnp.transpose(grad_key, (2, 0, 1)),
        grad_value.reshape(2 * N, 1, V),
        grad_square.reshape(()),
    )


def solution(mesh):
    grid = Mesh(mesh.devices.reshape(4, 4, 2, 16), ("x", "y", "c", "key"))
    in_specs = (
        P(SEQ, None, "key"),
        P(SEQ, None, "key"),
        P(SEQ, "key", None),
        P(SEQ, "key", None),
        P("key", SEQ),
        P("key", SEQ),
        P(SEQ, "key", None, None),
        P(SEQ, None, "key", None),
    )
    out_specs = (P(SEQ, None, "key"), P(SEQ, None, "key"), P(SEQ, "key", None), P())
    return jax.shard_map(local, mesh=grid, in_specs=in_specs, out_specs=out_specs, check_vma=False)
```

```python
import jax
import jax.numpy as jnp
from jax import lax
from jax.experimental import pallas as pl
from jax.experimental.pallas import tpu as pltpu
from jax.sharding import Mesh, PartitionSpec as P

F32 = jnp.float32
BF16 = jnp.bfloat16
SEQ = ("x", "y", "c")
N = 128
K = 256
V = 256
HALF = V // 2
PAD = 16
ROWS = K + PAD
HIDING = 6 * 10**10


def nn(a, b):
    return lax.dot_general(a, b, (((1,), (0,)), ((), ())), preferred_element_type=F32)


def nt(a, b):
    return lax.dot_general(a, b, (((1,), (1,)), ((), ())), preferred_element_type=F32)


def tn(a, b):
    return lax.dot_general(a, b, (((0,), (0,)), ((), ())), preferred_element_type=F32)


def split(a):
    high = a.astype(BF16)
    return high, (a - high.astype(F32)).astype(BF16)


def nn2(a, b):
    high, low = split(b)
    return nn(a, high) + nn(a, low)


def tn2(a, b):
    high, low = split(b)
    return tn(a, high) + tn(a, low)


def gates_of(gate_row, rate_row):
    rows = lax.broadcasted_iota(jnp.int32, (N, N), 0)
    cols = lax.broadcasted_iota(jnp.int32, (N, N), 1)
    lower = cols <= rows
    eye = cols == rows
    gate_col = jnp.sum(jnp.where(eye, gate_row, 0.0), axis=1, keepdims=True)
    rate_col = jnp.sum(jnp.where(eye, rate_row, 0.0), axis=1, keepdims=True)
    gamma_col = jnp.sum(jnp.where(lower, gate_row, 0.0), axis=1, keepdims=True)
    gamma_row = jnp.sum(jnp.where(rows <= cols, gate_col, 0.0), axis=0, keepdims=True)
    gamma_end = jnp.sum(gate_row, axis=1, keepdims=True)
    spread = jnp.where(lower, gamma_col - gamma_row, 0.0)
    mask = jnp.where(lower, jnp.exp(spread), 0.0)
    return gamma_row, gamma_end, mask, rate_col


def compose(first, second):
    decay1, m1, b1 = first
    decay2, m2, b2 = second
    both = nn(m1.astype(BF16), jnp.concatenate([m2, b2], axis=1).astype(BF16))
    return decay1 * decay2, decay2 * m1 + decay1 * m2 - both[:, :K], decay1 * b2 + b1 - both[:, K:]


def apply(first, state):
    decay, m, b = first
    return decay * state + b - nn(m.astype(BF16), state.astype(BF16))


def decay_rows(decay, width):
    high = decay.astype(BF16).astype(F32)
    middle = (decay - high).astype(BF16).astype(F32)
    low = decay - high - middle
    rows = lax.broadcasted_iota(jnp.int32, (PAD, width), 0)
    return jnp.where(rows == 0, high, jnp.where(rows == 1, middle, jnp.where(rows == 2, low, 0.0))).astype(BF16)


def decay_from(block):
    return jnp.sum(block.astype(F32), axis=0, keepdims=True)[:, :1]


def unpack(block):
    return decay_from(block[K:]), block[:K, :K].astype(F32), block[:K, K:].astype(F32)


def pack(ref, decayed):
    decay, m, b = decayed
    ref[:K, :K] = m.astype(BF16)
    ref[:K, K:] = b.astype(BF16)
    ref[K:, :] = decay_rows(decay, ref.shape[1])


def choose(flag, if_set, if_not):
    return tuple(jnp.where(flag, p, q) for p, q in zip(if_set, if_not))


def head_rows(kq_ref, which):
    return kq_ref[:, 16 * which : 16 * which + 16, :].reshape(K, 2 * N)


def local_map_kernel(kq_ref, grad_ref, gate_ref, rate_ref, inv_ref, map_ref, wt_ref, lg_ref):
    key_t = head_rows(kq_ref, 0)
    query_t = head_rows(kq_ref, 1)
    maps = []
    for g in range(2):
        span = slice(g * N, (g + 1) * N)
        rate = rate_ref[:, span]
        gamma, gamma_end, mask, _ = gates_of(gate_ref[:, span], rate)
        kt, qt = key_t[:, span], query_t[:, span]
        into = jnp.exp(gamma)
        scaled = (kt * (rate * into)).astype(BF16)
        wt = nt(scaled, inv_ref[g, 0]).astype(BF16)
        wt_ref[:, span] = wt
        score = (tn(qt, kt) * mask).astype(BF16)
        out_t = (kt * jnp.exp(gamma_end - gamma)).astype(BF16)
        in_t = (qt * into).astype(BF16)
        grad = grad_ref[span, :]
        lg = tn(score, grad)
        lg_ref[span, :] = lg
        offset = nn(in_t, grad) - nn2(wt, lg)
        maps.append((jnp.exp(gamma_end), nt(wt, out_t), offset))
    pack(map_ref, compose(*maps))


def pair_kernel(place_ref, own_ref, other_ref, map_ref):
    upper = place_ref[0] == 1

    def half(ref):
        decay, m, b = unpack(ref[...])
        return decay, m, jnp.where(upper, b[:, HALF:], b[:, :HALF])

    own, other = half(own_ref), half(other_ref)
    pack(map_ref, compose(choose(upper, other, own), choose(upper, own, other)))


def plane_kernel(place_ref, chips_ref, send_ref, end_ref, end_b_ref):
    suffix = unpack(chips_ref[3])
    end = (jnp.ones((1, 1), F32), jnp.zeros((K, K), F32), jnp.zeros((K, HALF), F32))
    for j in (2, 1, 0):
        end = choose(place_ref[1] == j, suffix, end)
        suffix = compose(unpack(chips_ref[j]), suffix)
    decay, m, b = suffix
    m_half = jnp.where(place_ref[0] == 0, m[:, :HALF], m[:, HALF:])
    send_ref[:K, :HALF] = m_half.astype(BF16)
    send_ref[:K, HALF:] = b.astype(BF16)
    send_ref[K:, :] = decay_rows(decay, 2 * HALF)
    decay, m, b = end
    end_ref[:K, :] = m
    end_ref[K:, :] = jnp.broadcast_to(decay, (8, K))
    end_b_ref[...] = b.astype(BF16)


def ahead_kernel(kq_ref, grad_ref, gate_ref, rate_ref, inv_ref, wt_ref, value_ref, state_ref,
                 gq_ref, nv_ref, ct_ref, sum_ref):
    key_t = head_rows(kq_ref, 0)
    query_t = head_rows(kq_ref, 1)
    total = jnp.zeros((1, 1), F32)
    for g in range(2):
        span = slice(g * N, (g + 1) * N)
        gamma, _, mask, rate_col = gates_of(gate_ref[:, span], rate_ref[:, span])
        kt, qt = key_t[:, span], query_t[:, span]
        state = state_ref[:, g].reshape(K, V)
        grad = grad_ref[span, :]
        scaled = (value_ref[span, :] * rate_col).astype(BF16)
        fresh = (nn(inv_ref[g, 0], scaled) - tn(wt_ref[:, span], state)).astype(BF16)
        nv_ref[span, :] = fresh
        score = (nt(grad, fresh) * mask).astype(BF16)
        gq = (jnp.exp(gamma) * nt(state, grad) + nt(kt, score)).astype(BF16)
        gq_ref[:, :, span] = gq.reshape(16, 16, N)
        ct_ref[:, span] = nn(qt, score)
        total += jnp.sum(jnp.square(gq.astype(F32)), keepdims=True)
    sum_ref[...] = jnp.broadcast_to(total, (8, 128))


def state_after(place_ref, halves_ref, end_ref, other_ref):
    low, high = (halves_ref[i, 2 * ROWS :, :].astype(F32) for i in range(2))
    state = jnp.concatenate([low[:, :HALF], high[:, :HALF]], axis=1)
    end_b = jnp.concatenate([low[:, HALF:], high[:, HALF:]], axis=1)
    for d in (1, 0):
        low, high = (halves_ref[i, ROWS * d : ROWS * (d + 1), :] for i in range(2))
        m = jnp.concatenate([low[:K, :HALF], high[:K, :HALF]], axis=1)
        b = jnp.concatenate([low[:K, HALF:], high[:K, HALF:]], axis=1).astype(F32)
        state = apply((decay_from(low[K:]), m, b), state)
    state = apply((end_ref[K : K + 1, :1], end_ref[:K, :], end_b), state)
    return jnp.where(place_ref[0] == 0, apply(unpack(other_ref[...]), state), state)


def final_kernel(place_ref, halves_ref, end_ref, other_ref, kq_ref, grad_ref, gate_ref, rate_ref, inv_ref, wt_ref,
                 lg_ref, state_ref, nv_ref, ct_ref, sum_ref, gq_ref, out_ref, gv_ref):
    key_t = head_rows(kq_ref, 0)
    query_t = head_rows(kq_ref, 1)
    state_grad = state_after(place_ref, halves_ref, end_ref, other_ref)
    total = sum_ref[:1, :1]
    for g in (1, 0):
        span = slice(g * N, (g + 1) * N)
        rate = rate_ref[:, span]
        gamma, gamma_end, _, rate_col = gates_of(gate_ref[:, span], rate)
        into = jnp.exp(gamma)
        away = jnp.exp(gamma_end - gamma)
        inverse = inv_ref[g, 0]
        out_t = (key_t[:, span] * away).astype(BF16)
        high, low = split(state_grad)
        value_grad = lg_ref[span, :] + tn(out_t, high) + tn(out_t, low)
        rounded = value_grad.astype(BF16)
        gv = (rate_col * tn(inverse, rounded)).astype(BF16)
        gv_ref[span, :] = gv
        write_t = (-nt(state_ref[:, g].reshape(K, V), rounded)).astype(BF16)
        gk = (ct_ref[:, span] + away * nt(high, nv_ref[span, :]) + (rate * into) * nn(write_t, inverse)).astype(BF16)
        out_ref[:, 16 * g : 16 * g + 16, :] = gq_ref[:, :, span]
        out_ref[:, 32 + 16 * g : 48 + 16 * g, :] = gk.reshape(16, 16, N)
        total += jnp.sum(jnp.square(gk.astype(F32)), keepdims=True) + jnp.sum(
            jnp.square(gv.astype(F32)), keepdims=True
        )
        if g == 1:
            in_t = (query_t[:, span] * into).astype(BF16)
            state_grad = (
                jnp.exp(gamma_end) * state_grad
                + nn(in_t, grad_ref[span, :])
                - nn2(wt_ref[:, span], value_grad)
            )
    high = total.astype(BF16).astype(F32)
    middle = (total - high).astype(BF16).astype(F32)
    low = total - high - middle
    rows = lax.broadcasted_iota(jnp.int32, (16, N), 0)
    pieces = jnp.where(rows == 0, high, jnp.where(rows == 1, middle, jnp.where(rows == 2, low, 0.0)))
    out_ref[:, 64:, :] = jnp.broadcast_to(pieces.astype(BF16)[None], (16, 16, N))


def join_kernel(key_ref, query_ref, out_ref, done):
    copies = [
        pltpu.make_async_copy(ref, out_ref.at[:, pl.ds(16 * i, 16), :], done.at[i])
        for i, ref in enumerate((key_ref, query_ref))
    ]
    for copy in copies:
        copy.start()
    for copy in copies:
        copy.wait()


def join(keys, queries):
    spec = pl.BlockSpec(memory_space=pl.ANY)
    return pl.pallas_call(
        join_kernel,
        out_shape=shape((16, 32, 2 * N)),
        in_specs=[spec, spec],
        out_specs=pl.BlockSpec(memory_space=pltpu.VMEM),
        scratch_shapes=[pltpu.SemaphoreType.DMA((2,))],
    )(keys, queries)


def spread_kernel(back_ref, out_ref):
    pieces = jnp.sum(back_ref[:, 64:, :].astype(F32), axis=0)
    total = jnp.sum(pieces, axis=0, keepdims=True)
    out_ref[...] = jnp.broadcast_to(total[None], (32, 1, 128))


def receive_kernel(back_ref, gq_ref, gk_ref):
    for at, ref in ((0, gq_ref), (32, gk_ref)):
        ref[:, :, :N] = back_ref[:, at : at + 16, :]
        ref[:, :, N:] = back_ref[:, at + 16 : at + 32, :]


def call(kernel, outs, args, flops, scratch=(), scalars=0):
    spec = pl.BlockSpec(memory_space=pltpu.VMEM)
    smem = pl.BlockSpec(memory_space=pltpu.SMEM)
    moved = sum(a.size * a.dtype.itemsize for a in args)
    return pl.pallas_call(
        kernel,
        out_shape=outs,
        in_specs=[smem] * scalars + [spec] * (len(args) - scalars),
        out_specs=[spec] * len(outs),
        scratch_shapes=list(scratch),
        cost_estimate=pl.CostEstimate(flops=flops, bytes_accessed=moved, transcendentals=0),
        compiler_params=pltpu.CompilerParams(vmem_limit_bytes=24 * 2**20),
    )(*args)


def shape(dims, dtype=BF16):
    return jax.ShapeDtypeStruct(dims, dtype)


def to_heads(array):
    return lax.all_to_all(array, "key", 0, 0, tiled=True)


def local(query_rows, key_rows, value_rows, out_grad, log_gates, write_rate, group_inverse, states):
    keys = jnp.transpose(key_rows, (1, 2, 0))
    queries = jnp.transpose(query_rows, (1, 2, 0))
    kq = to_heads(join(keys, queries))
    grad = out_grad.reshape(2 * N, V)
    values = value_rows.reshape(2 * N, V)
    x, y, c = (lax.axis_index(name) for name in SEQ)
    place = jnp.stack([c, y, x]).astype(jnp.int32)
    chip_map = shape((K + PAD, K + HALF))
    square = shape((K, V), F32)
    basics = (kq, grad, log_gates, write_rate, group_inverse)

    device_map, written_t, local_grad = call(
        local_map_kernel, [shape((K + PAD, K + V)), shape((K, 2 * N)), square], basics, 10**8
    )
    state_blocks, device_map = lax.optimization_barrier((jnp.transpose(states, (1, 0, 2, 3)), device_map))
    state_heads = to_heads(state_blocks)
    chip_other = lax.ppermute(device_map, "c", [(0, 1), (1, 0)])
    (now,) = call(pair_kernel, [chip_map], (place, device_map, chip_other), HIDING, scalars=1)
    plane_half, end, end_b = call(
        plane_kernel,
        [shape((ROWS, 2 * HALF)), shape((K + 8, K), F32), shape((K, HALF))],
        (place, lax.all_gather(now, "y")),
        10**8,
        scalars=1,
    )
    later = [lax.ppermute(plane_half, "x", [(s, s - d) for s in range(d, 4)]) for d in (1, 2, 3)]

    gq, fresh, score_term, query_sum = call(
        ahead_kernel,
        [shape((16, 16, 2 * N)), shape((2 * N, V)), square, shape((8, 128), F32)],
        (*basics, written_t, values, state_heads),
        2 * 10**8,
    )
    later, fresh = lax.optimization_barrier((later, fresh))
    last = jnp.concatenate([later[2][:K, HALF:], end_b], axis=1)
    halves = lax.all_gather(jnp.concatenate([later[0], later[1], last], axis=0), "c")
    sent, grad_value = call(
        final_kernel,
        [shape((16, 80, N)), shape((2 * N, V))],
        (
            place, halves, end, chip_other, *basics, written_t, local_grad, state_heads, fresh, score_term,
            query_sum, gq,
        ),
        4 * 10**8,
        scalars=1,
    )
    back = to_heads(sent)
    (spread,) = call(spread_kernel, [shape((32, 1, 128), F32)], (back,), 10**6)
    parts = lax.all_to_all(spread, SEQ, 0, 0, tiled=True)
    grad_square = jnp.sum(parts[:, 0, 0]) / (8192 * 16 * (2 * K + V))
    grad_query, grad_key = call(receive_kernel, [shape((16, 16, 2 * N))] * 2, (back,), 10**6)
    return (
        jnp.transpose(grad_query, (2, 0, 1)),
        jnp.transpose(grad_key, (2, 0, 1)),
        grad_value.reshape(2 * N, 1, V),
        grad_square,
    )


def solution(mesh):
    grid = Mesh(mesh.devices.reshape(4, 4, 2, 16), ("x", "y", "c", "key"))
    in_specs = (
        P(SEQ, None, "key"),
        P(SEQ, None, "key"),
        P(SEQ, "key", None),
        P(SEQ, "key", None),
        P("key", SEQ),
        P("key", SEQ),
        P(SEQ, "key", None, None),
        P(SEQ, None, "key", None),
    )
    out_specs = (P(SEQ, None, "key"), P(SEQ, None, "key"), P(SEQ, "key", None), P())
    return jax.shard_map(local, mesh=grid, in_specs=in_specs, out_specs=out_specs, check_vma=False)
```

```python
import jax
import jax.numpy as jnp
from jax import lax
from jax.experimental import pallas as pl
from jax.experimental.pallas import tpu as pltpu
from jax.sharding import Mesh, PartitionSpec as P

F32 = jnp.float32
BF16 = jnp.bfloat16
SEQ = ("x", "y", "c")
N = 128
K = 256
V = 256
HALF = V // 2
PAD = 16
ROWS = K + PAD
HIDING = 6 * 10**10


def nn(a, b):
    return lax.dot_general(a, b, (((1,), (0,)), ((), ())), preferred_element_type=F32)


def nt(a, b):
    return lax.dot_general(a, b, (((1,), (1,)), ((), ())), preferred_element_type=F32)


def tn(a, b):
    return lax.dot_general(a, b, (((0,), (0,)), ((), ())), preferred_element_type=F32)


def split(a):
    high = a.astype(BF16)
    return high, (a - high.astype(F32)).astype(BF16)


def nn2(a, b):
    high, low = split(b)
    return nn(a, high) + nn(a, low)


def tn2(a, b):
    high, low = split(b)
    return tn(a, high) + tn(a, low)


def gates_of(gate_row, rate_row):
    rows = lax.broadcasted_iota(jnp.int32, (N, N), 0)
    cols = lax.broadcasted_iota(jnp.int32, (N, N), 1)
    lower = cols <= rows
    eye = cols == rows
    gate_col = jnp.sum(jnp.where(eye, gate_row, 0.0), axis=1, keepdims=True)
    rate_col = jnp.sum(jnp.where(eye, rate_row, 0.0), axis=1, keepdims=True)
    gamma_col = jnp.sum(jnp.where(lower, gate_row, 0.0), axis=1, keepdims=True)
    gamma_row = jnp.sum(jnp.where(rows <= cols, gate_col, 0.0), axis=0, keepdims=True)
    gamma_end = jnp.sum(gate_row, axis=1, keepdims=True)
    spread = jnp.where(lower, gamma_col - gamma_row, 0.0)
    mask = jnp.where(lower, jnp.exp(spread), 0.0)
    return gamma_row, gamma_end, mask, rate_col


def compose(first, second):
    decay1, m1, b1 = first
    decay2, m2, b2 = second
    both = nn(m1.astype(BF16), jnp.concatenate([m2, b2], axis=1).astype(BF16))
    return decay1 * decay2, decay2 * m1 + decay1 * m2 - both[:, :K], decay1 * b2 + b1 - both[:, K:]


def apply(first, state):
    decay, m, b = first
    return decay * state + b - nn(m.astype(BF16), state.astype(BF16))


def decay_rows(decay, width):
    high = decay.astype(BF16).astype(F32)
    middle = (decay - high).astype(BF16).astype(F32)
    low = decay - high - middle
    rows = lax.broadcasted_iota(jnp.int32, (PAD, width), 0)
    return jnp.where(rows == 0, high, jnp.where(rows == 1, middle, jnp.where(rows == 2, low, 0.0))).astype(BF16)


def decay_from(block):
    return jnp.sum(block.astype(F32), axis=0, keepdims=True)[:, :1]


def unpack(block):
    return decay_from(block[K:]), block[:K, :K].astype(F32), block[:K, K:].astype(F32)


def pack(ref, decayed):
    decay, m, b = decayed
    ref[:K, :K] = m.astype(BF16)
    ref[:K, K:] = b.astype(BF16)
    ref[K:, :] = decay_rows(decay, ref.shape[1])


def choose(flag, if_set, if_not):
    return tuple(jnp.where(flag, p, q) for p, q in zip(if_set, if_not))


def head_rows(kq_ref, which):
    return kq_ref[:, 16 * which : 16 * which + 16, :].reshape(K, 2 * N)


def local_map_kernel(kq_ref, grad_ref, gate_ref, rate_ref, inv_ref, map_ref, wt_ref, lg_ref):
    key_t = head_rows(kq_ref, 0)
    query_t = head_rows(kq_ref, 1)
    maps = []
    for g in range(2):
        span = slice(g * N, (g + 1) * N)
        rate = rate_ref[:, span]
        gamma, gamma_end, mask, _ = gates_of(gate_ref[:, span], rate)
        kt, qt = key_t[:, span], query_t[:, span]
        into = jnp.exp(gamma)
        scaled = (kt * (rate * into)).astype(BF16)
        wt = nt(scaled, inv_ref[g, 0]).astype(BF16)
        wt_ref[:, span] = wt
        score = (tn(qt, kt) * mask).astype(BF16)
        out_t = (kt * jnp.exp(gamma_end - gamma)).astype(BF16)
        in_t = (qt * into).astype(BF16)
        grad = grad_ref[span, :]
        lg = tn(score, grad)
        lg_ref[span, :] = lg
        offset = nn(in_t, grad) - nn2(wt, lg)
        maps.append((jnp.exp(gamma_end), nt(wt, out_t), offset))
    pack(map_ref, compose(*maps))


def pair_kernel(place_ref, own_ref, other_ref, map_ref):
    upper = place_ref[0] == 1

    def half(ref):
        decay, m, b = unpack(ref[...])
        return decay, m, jnp.where(upper, b[:, HALF:], b[:, :HALF])

    own, other = half(own_ref), half(other_ref)
    pack(map_ref, compose(choose(upper, other, own), choose(upper, own, other)))


def plane_kernel(place_ref, chips_ref, send_ref, end_ref, end_b_ref):
    suffix = unpack(chips_ref[3])
    end = (jnp.ones((1, 1), F32), jnp.zeros((K, K), F32), jnp.zeros((K, HALF), F32))
    for j in (2, 1, 0):
        end = choose(place_ref[1] == j, suffix, end)
        suffix = compose(unpack(chips_ref[j]), suffix)
    decay, m, b = suffix
    m_half = jnp.where(place_ref[0] == 0, m[:, :HALF], m[:, HALF:])
    send_ref[:K, :HALF] = m_half.astype(BF16)
    send_ref[:K, HALF:] = b.astype(BF16)
    send_ref[K:, :] = decay_rows(decay, 2 * HALF)
    decay, m, b = end
    end_ref[:K, :] = m
    end_ref[K:, :] = jnp.broadcast_to(decay, (8, K))
    end_b_ref[...] = b.astype(BF16)


def ahead_kernel(kq_ref, grad_ref, gate_ref, rate_ref, inv_ref, wt_ref, value_ref, state_ref,
                 gq_ref, nv_ref, ct_ref, sum_ref):
    key_t = head_rows(kq_ref, 0)
    query_t = head_rows(kq_ref, 1)
    total = jnp.zeros((1, 1), F32)
    for g in range(2):
        span = slice(g * N, (g + 1) * N)
        gamma, _, mask, rate_col = gates_of(gate_ref[:, span], rate_ref[:, span])
        kt, qt = key_t[:, span], query_t[:, span]
        state = state_ref[:, g].reshape(K, V)
        grad = grad_ref[span, :]
        scaled = (value_ref[span, :] * rate_col).astype(BF16)
        fresh = (nn(inv_ref[g, 0], scaled) - tn(wt_ref[:, span], state)).astype(BF16)
        nv_ref[span, :] = fresh
        score = (nt(grad, fresh) * mask).astype(BF16)
        gq = (jnp.exp(gamma) * nt(state, grad) + nt(kt, score)).astype(BF16)
        gq_ref[:, :, span] = gq.reshape(16, 16, N)
        ct_ref[:, span] = nn(qt, score)
        total += jnp.sum(jnp.square(gq.astype(F32)), keepdims=True)
    sum_ref[...] = jnp.broadcast_to(total, (8, 128))


def state_after(place_ref, halves_ref, end_ref, other_ref):
    low, high = (halves_ref[i, 2 * ROWS :, :].astype(F32) for i in range(2))
    state = jnp.concatenate([low[:, :HALF], high[:, :HALF]], axis=1)
    end_b = jnp.concatenate([low[:, HALF:], high[:, HALF:]], axis=1)
    for d in (1, 0):
        low, high = (halves_ref[i, ROWS * d : ROWS * (d + 1), :] for i in range(2))
        m = jnp.concatenate([low[:K, :HALF], high[:K, :HALF]], axis=1)
        b = jnp.concatenate([low[:K, HALF:], high[:K, HALF:]], axis=1).astype(F32)
        state = apply((decay_from(low[K:]), m, b), state)
    state = apply((end_ref[K : K + 1, :1], end_ref[:K, :], end_b), state)
    return jnp.where(place_ref[0] == 0, apply(unpack(other_ref[...]), state), state)


def final_kernel(place_ref, halves_ref, end_ref, other_ref, kq_ref, grad_ref, gate_ref, rate_ref, inv_ref, wt_ref,
                 lg_ref, state_ref, nv_ref, ct_ref, sum_ref, gk_ref, gv_ref, total_ref):
    key_t = head_rows(kq_ref, 0)
    query_t = head_rows(kq_ref, 1)
    state_grad = state_after(place_ref, halves_ref, end_ref, other_ref)
    total = sum_ref[:1, :1]
    for g in (1, 0):
        span = slice(g * N, (g + 1) * N)
        rate = rate_ref[:, span]
        gamma, gamma_end, _, rate_col = gates_of(gate_ref[:, span], rate)
        into = jnp.exp(gamma)
        away = jnp.exp(gamma_end - gamma)
        inverse = inv_ref[g, 0]
        out_t = (key_t[:, span] * away).astype(BF16)
        high, low = split(state_grad)
        value_grad = lg_ref[span, :] + tn(out_t, high) + tn(out_t, low)
        rounded = value_grad.astype(BF16)
        gv = (rate_col * tn(inverse, rounded)).astype(BF16)
        gv_ref[span, :] = gv
        write_t = (-nt(state_ref[:, g].reshape(K, V), rounded)).astype(BF16)
        gk = (ct_ref[:, span] + away * nt(high, nv_ref[span, :]) + (rate * into) * nn(write_t, inverse)).astype(BF16)
        gk_ref[:, :, span] = gk.reshape(16, 16, N)
        total += jnp.sum(jnp.square(gk.astype(F32)), keepdims=True) + jnp.sum(
            jnp.square(gv.astype(F32)), keepdims=True
        )
        if g == 1:
            in_t = (query_t[:, span] * into).astype(BF16)
            state_grad = (
                jnp.exp(gamma_end) * state_grad
                + nn(in_t, grad_ref[span, :])
                - nn2(wt_ref[:, span], value_grad)
            )
    total_ref[...] = jnp.broadcast_to(total[None], (32, 1, 128))


def join_kernel(key_ref, query_ref, out_ref, done):
    copies = [
        pltpu.make_async_copy(ref, out_ref.at[:, pl.ds(16 * i, 16), :], done.at[i])
        for i, ref in enumerate((key_ref, query_ref))
    ]
    for copy in copies:
        copy.start()
    for copy in copies:
        copy.wait()


def join(keys, queries):
    spec = pl.BlockSpec(memory_space=pl.ANY)
    return pl.pallas_call(
        join_kernel,
        out_shape=shape((16, 32, 2 * N)),
        in_specs=[spec, spec],
        out_specs=pl.BlockSpec(memory_space=pltpu.VMEM),
        scratch_shapes=[pltpu.SemaphoreType.DMA((2,))],
    )(keys, queries)


def send_kernel(gq_ref, gk_ref, parts_ref, out_ref):
    total = jnp.sum(parts_ref[...], axis=0)
    high = total.astype(BF16).astype(F32)
    middle = (total - high).astype(BF16).astype(F32)
    low = total - high - middle
    rows = lax.broadcasted_iota(jnp.int32, (16, N), 0)
    pieces = jnp.where(rows == 0, high, jnp.where(rows == 1, middle, jnp.where(rows == 2, low, 0.0)))
    for at, ref in ((0, gq_ref), (32, gk_ref)):
        out_ref[:, at : at + 16, :] = ref[:, :, :N]
        out_ref[:, at + 16 : at + 32, :] = ref[:, :, N:]
    out_ref[:, 64:, :] = jnp.broadcast_to(pieces.astype(BF16)[None], (16, 16, N))


def receive_kernel(back_ref, gq_ref, gk_ref, square_ref):
    for at, ref in ((0, gq_ref), (32, gk_ref)):
        ref[:, :, :N] = back_ref[:, at : at + 16, :]
        ref[:, :, N:] = back_ref[:, at + 16 : at + 32, :]
    pieces = jnp.sum(back_ref[:, 64:, :].astype(F32), axis=0)
    total = jnp.sum(pieces, axis=0, keepdims=True)
    square_ref[...] = total[:, :1] * (1.0 / (8192 * 16 * (2 * K + V)))


def call(kernel, outs, args, flops, scratch=(), scalars=0):
    spec = pl.BlockSpec(memory_space=pltpu.VMEM)
    smem = pl.BlockSpec(memory_space=pltpu.SMEM)
    moved = sum(a.size * a.dtype.itemsize for a in args)
    return pl.pallas_call(
        kernel,
        out_shape=outs,
        in_specs=[smem] * scalars + [spec] * (len(args) - scalars),
        out_specs=[spec] * len(outs),
        scratch_shapes=list(scratch),
        cost_estimate=pl.CostEstimate(flops=flops, bytes_accessed=moved, transcendentals=0),
        compiler_params=pltpu.CompilerParams(vmem_limit_bytes=24 * 2**20),
    )(*args)


def shape(dims, dtype=BF16):
    return jax.ShapeDtypeStruct(dims, dtype)


def to_heads(array):
    return lax.all_to_all(array, "key", 0, 0, tiled=True)


def local(query_rows, key_rows, value_rows, out_grad, log_gates, write_rate, group_inverse, states):
    keys = jnp.transpose(key_rows, (1, 2, 0))
    queries = jnp.transpose(query_rows, (1, 2, 0))
    kq = to_heads(join(keys, queries))
    grad = out_grad.reshape(2 * N, V)
    values = value_rows.reshape(2 * N, V)
    x, y, c = (lax.axis_index(name) for name in SEQ)
    place = jnp.stack([c, y, x]).astype(jnp.int32)
    chip_map = shape((K + PAD, K + HALF))
    square = shape((K, V), F32)
    basics = (kq, grad, log_gates, write_rate, group_inverse)

    device_map, written_t, local_grad = call(
        local_map_kernel, [shape((K + PAD, K + V)), shape((K, 2 * N)), square], basics, 10**8
    )
    state_blocks, device_map = lax.optimization_barrier((jnp.transpose(states, (1, 0, 2, 3)), device_map))
    state_heads = to_heads(state_blocks)
    chip_other = lax.ppermute(device_map, "c", [(0, 1), (1, 0)])
    (now,) = call(pair_kernel, [chip_map], (place, device_map, chip_other), HIDING, scalars=1)
    plane_half, end, end_b = call(
        plane_kernel,
        [shape((ROWS, 2 * HALF)), shape((K + 8, K), F32), shape((K, HALF))],
        (place, lax.all_gather(now, "y")),
        10**8,
        scalars=1,
    )
    later = [lax.ppermute(plane_half, "x", [(s, s - d) for s in range(d, 4)]) for d in (1, 2, 3)]

    gq, fresh, score_term, query_sum = call(
        ahead_kernel,
        [shape((16, 16, 2 * N)), shape((2 * N, V)), square, shape((8, 128), F32)],
        (*basics, written_t, values, state_heads),
        2 * 10**8,
    )
    later, fresh = lax.optimization_barrier((later, fresh))
    last = jnp.concatenate([later[2][:K, HALF:], end_b], axis=1)
    halves = lax.all_gather(jnp.concatenate([later[0], later[1], last], axis=0), "c")
    gk, grad_value, total = call(
        final_kernel,
        [shape((16, 16, 2 * N)), shape((2 * N, V)), shape((32, 1, 128), F32)],
        (
            place, halves, end, chip_other, *basics, written_t, local_grad, state_heads, fresh, score_term,
            query_sum,
        ),
        4 * 10**8,
        scalars=1,
    )
    parts = lax.all_to_all(total, SEQ, 0, 0, tiled=True)
    (sent,) = call(send_kernel, [shape((16, 80, N))], (gq, gk, parts), 10**6)
    grad_query, grad_key, grad_square = call(
        receive_kernel,
        [shape((16, 16, 2 * N)), shape((16, 16, 2 * N)), shape((1, 1), F32)],
        (to_heads(sent),),
        10**6,
    )
    return (
        jnp.transpose(grad_query, (2, 0, 1)),
        jnp.transpose(grad_key, (2, 0, 1)),
        grad_value.reshape(2 * N, 1, V),
        grad_square.reshape(()),
    )


def solution(mesh):
    grid = Mesh(mesh.devices.reshape(4, 4, 2, 16), ("x", "y", "c", "key"))
    in_specs = (
        P(SEQ, None, "key"),
        P(SEQ, None, "key"),
        P(SEQ, "key", None),
        P(SEQ, "key", None),
        P("key", SEQ),
        P("key", SEQ),
        P(SEQ, "key", None, None),
        P(SEQ, None, "key", None),
    )
    out_specs = (P(SEQ, None, "key"), P(SEQ, None, "key"), P(SEQ, "key", None), P())
    return jax.shard_map(local, mesh=grid, in_specs=in_specs, out_specs=out_specs, check_vma=False)
```

```python
import jax
import jax.numpy as jnp
from jax import lax
from jax.experimental import pallas as pl
from jax.experimental.pallas import tpu as pltpu
from jax.sharding import Mesh, PartitionSpec as P

F32 = jnp.float32
BF16 = jnp.bfloat16
SEQ = ("x", "y", "c")
N = 128
K = 256
V = 256
HALF = V // 2
PAD = 16
ROWS = K + PAD
HIDING = 6 * 10**10


def nn(a, b):
    return lax.dot_general(a, b, (((1,), (0,)), ((), ())), preferred_element_type=F32)


def nt(a, b):
    return lax.dot_general(a, b, (((1,), (1,)), ((), ())), preferred_element_type=F32)


def tn(a, b):
    return lax.dot_general(a, b, (((0,), (0,)), ((), ())), preferred_element_type=F32)


def split(a):
    high = a.astype(BF16)
    return high, (a - high.astype(F32)).astype(BF16)


def nn2(a, b):
    high, low = split(b)
    return nn(a, high) + nn(a, low)


def tn2(a, b):
    high, low = split(b)
    return tn(a, high) + tn(a, low)


def gates_of(gate_row, rate_row):
    rows = lax.broadcasted_iota(jnp.int32, (N, N), 0)
    cols = lax.broadcasted_iota(jnp.int32, (N, N), 1)
    lower = cols <= rows
    eye = cols == rows
    gate_col = jnp.sum(jnp.where(eye, gate_row, 0.0), axis=1, keepdims=True)
    rate_col = jnp.sum(jnp.where(eye, rate_row, 0.0), axis=1, keepdims=True)
    gamma_col = jnp.sum(jnp.where(lower, gate_row, 0.0), axis=1, keepdims=True)
    gamma_row = jnp.sum(jnp.where(rows <= cols, gate_col, 0.0), axis=0, keepdims=True)
    gamma_end = jnp.sum(gate_row, axis=1, keepdims=True)
    spread = jnp.where(lower, gamma_col - gamma_row, 0.0)
    mask = jnp.where(lower, jnp.exp(spread), 0.0)
    return gamma_row, gamma_end, mask, rate_col


def compose(first, second):
    decay1, m1, b1 = first
    decay2, m2, b2 = second
    both = nn(m1.astype(BF16), jnp.concatenate([m2, b2], axis=1).astype(BF16))
    return decay1 * decay2, decay2 * m1 + decay1 * m2 - both[:, :K], decay1 * b2 + b1 - both[:, K:]


def apply(first, state):
    decay, m, b = first
    return decay * state + b - nn(m.astype(BF16), state.astype(BF16))


def decay_rows(decay, width):
    high = decay.astype(BF16).astype(F32)
    middle = (decay - high).astype(BF16).astype(F32)
    low = decay - high - middle
    rows = lax.broadcasted_iota(jnp.int32, (PAD, width), 0)
    return jnp.where(rows == 0, high, jnp.where(rows == 1, middle, jnp.where(rows == 2, low, 0.0))).astype(BF16)


def decay_from(block):
    return jnp.sum(block.astype(F32), axis=0, keepdims=True)[:, :1]


def unpack(block):
    return decay_from(block[K:]), block[:K, :K].astype(F32), block[:K, K:].astype(F32)


def pack(ref, decayed):
    decay, m, b = decayed
    ref[:K, :K] = m.astype(BF16)
    ref[:K, K:] = b.astype(BF16)
    ref[K:, :] = decay_rows(decay, ref.shape[1])


def choose(flag, if_set, if_not):
    return tuple(jnp.where(flag, p, q) for p, q in zip(if_set, if_not))


def head_rows(kq_ref, which):
    return kq_ref[:, 16 * which : 16 * which + 16, :].reshape(K, 2 * N)


def local_map_kernel(kq_ref, grad_ref, gate_ref, rate_ref, inv_ref, map_ref, wt_ref, lg_ref, later_m_ref, later_b_ref):
    key_t = head_rows(kq_ref, 0)
    query_t = head_rows(kq_ref, 1)
    maps = []
    for g in range(2):
        span = slice(g * N, (g + 1) * N)
        rate = rate_ref[:, span]
        gamma, gamma_end, mask, _ = gates_of(gate_ref[:, span], rate)
        kt, qt = key_t[:, span], query_t[:, span]
        into = jnp.exp(gamma)
        scaled = (kt * (rate * into)).astype(BF16)
        wt = nt(scaled, inv_ref[g, 0]).astype(BF16)
        wt_ref[:, span] = wt
        score = (tn(qt, kt) * mask).astype(BF16)
        out_t = (kt * jnp.exp(gamma_end - gamma)).astype(BF16)
        in_t = (qt * into).astype(BF16)
        grad = grad_ref[span, :]
        lg = tn(score, grad)
        lg_ref[span, :] = lg
        offset = nn(in_t, grad) - nn2(wt, lg)
        maps.append((jnp.exp(gamma_end), nt(wt, out_t), offset))
    pack(map_ref, compose(*maps))
    later_m_ref[...] = maps[1][1].astype(BF16)
    later_b_ref[...] = maps[1][2]


def pair_kernel(place_ref, own_ref, other_ref, map_ref):
    upper = place_ref[0] == 1

    def half(ref):
        decay, m, b = unpack(ref[...])
        return decay, m, jnp.where(upper, b[:, HALF:], b[:, :HALF])

    own, other = half(own_ref), half(other_ref)
    pack(map_ref, compose(choose(upper, other, own), choose(upper, own, other)))


def plane_kernel(place_ref, chips_ref, send_ref, send_b_ref, end_ref, end_b_ref):
    suffix = unpack(chips_ref[3])
    end = (jnp.ones((1, 1), F32), jnp.zeros((K, K), F32), jnp.zeros((K, HALF), F32))
    for j in (2, 1, 0):
        end = choose(place_ref[1] == j, suffix, end)
        suffix = compose(unpack(chips_ref[j]), suffix)
    decay, m, b = suffix
    m_half = jnp.where(place_ref[0] == 0, m[:, :HALF], m[:, HALF:])
    send_ref[:K, :HALF] = m_half.astype(BF16)
    send_ref[:K, HALF:] = b.astype(BF16)
    send_ref[K:, :] = decay_rows(decay, 2 * HALF)
    send_b_ref[...] = b.astype(BF16)
    decay, m, b = end
    end_ref[:K, :] = m
    end_ref[K:, :] = jnp.broadcast_to(decay, (8, K))
    end_b_ref[...] = b.astype(BF16)


def ahead_kernel(kq_ref, grad_ref, gate_ref, rate_ref, inv_ref, wt_ref, value_ref, state_ref,
                 gq_ref, nv_ref, ct_ref, sum_ref):
    key_t = head_rows(kq_ref, 0)
    query_t = head_rows(kq_ref, 1)
    total = jnp.zeros((1, 1), F32)
    for g in range(2):
        span = slice(g * N, (g + 1) * N)
        gamma, _, mask, rate_col = gates_of(gate_ref[:, span], rate_ref[:, span])
        kt, qt = key_t[:, span], query_t[:, span]
        state = state_ref[:, g].reshape(K, V)
        grad = grad_ref[span, :]
        scaled = (value_ref[span, :] * rate_col).astype(BF16)
        fresh = (nn(inv_ref[g, 0], scaled) - tn(wt_ref[:, span], state)).astype(BF16)
        nv_ref[span, :] = fresh
        score = (nt(grad, fresh) * mask).astype(BF16)
        gq = (jnp.exp(gamma) * nt(state, grad) + nt(kt, score)).astype(BF16)
        gq_ref[:, :, span] = gq.reshape(16, 16, N)
        ct_ref[:, span] = nn(qt, score)
        total += jnp.sum(jnp.square(gq.astype(F32)), keepdims=True)
    sum_ref[...] = jnp.broadcast_to(total, (8, 128))


def state_after(place_ref, halves_ref, end_ref, other_ref):
    low, high = (halves_ref[i, 2 * ROWS :, :].astype(F32) for i in range(2))
    state = jnp.concatenate([low[:, :HALF], high[:, :HALF]], axis=1)
    end_b = jnp.concatenate([low[:, HALF:], high[:, HALF:]], axis=1)
    for d in (1, 0):
        low, high = (halves_ref[i, ROWS * d : ROWS * (d + 1), :] for i in range(2))
        m = jnp.concatenate([low[:K, :HALF], high[:K, :HALF]], axis=1)
        b = jnp.concatenate([low[:K, HALF:], high[:K, HALF:]], axis=1).astype(F32)
        ahead = apply((decay_from(low[K:]), m, b), state)
        state = jnp.where(place_ref[2] == 1, state, ahead) if d == 1 else ahead
    state = apply((end_ref[K : K + 1, :1], end_ref[:K, :], end_b), state)
    return jnp.where(place_ref[0] == 0, apply(unpack(other_ref[...]), state), state)


def final_kernel(place_ref, halves_ref, end_ref, other_ref, later_m_ref, later_b_ref, kq_ref, gate_ref, rate_ref,
                 inv_ref, lg_ref, state_ref, nv_ref, ct_ref, sum_ref, gk_ref, gv_ref, total_ref):
    key_t = head_rows(kq_ref, 0)
    state_grad = state_after(place_ref, halves_ref, end_ref, other_ref)
    total = sum_ref[:1, :1]
    for g in (1, 0):
        span = slice(g * N, (g + 1) * N)
        rate = rate_ref[:, span]
        gamma, gamma_end, _, rate_col = gates_of(gate_ref[:, span], rate)
        into = jnp.exp(gamma)
        away = jnp.exp(gamma_end - gamma)
        inverse = inv_ref[g, 0]
        out_t = (key_t[:, span] * away).astype(BF16)
        high, low = split(state_grad)
        value_grad = lg_ref[span, :] + tn(out_t, high) + tn(out_t, low)
        rounded = value_grad.astype(BF16)
        gv = (rate_col * tn(inverse, rounded)).astype(BF16)
        gv_ref[span, :] = gv
        write_t = (-nt(state_ref[:, g].reshape(K, V), rounded)).astype(BF16)
        gk = (ct_ref[:, span] + away * nt(high, nv_ref[span, :]) + (rate * into) * nn(write_t, inverse)).astype(BF16)
        gk_ref[:, :, span] = gk.reshape(16, 16, N)
        total += jnp.sum(jnp.square(gk.astype(F32)), keepdims=True) + jnp.sum(
            jnp.square(gv.astype(F32)), keepdims=True
        )
        if g == 1:
            state_grad = apply((jnp.exp(gamma_end), later_m_ref[...], later_b_ref[...]), state_grad)
    total_ref[...] = jnp.broadcast_to(total[None], (32, 1, 128))


def join_kernel(key_ref, query_ref, out_ref, held, done):
    inward = [pltpu.make_async_copy(ref, held.at[i], done.at[i]) for i, ref in enumerate((key_ref, query_ref))]
    outward = [
        pltpu.make_async_copy(held.at[i], out_ref.at[:, pl.ds(16 * i, 16), :], done.at[2 + i]) for i in range(2)
    ]
    for copy in inward:
        copy.start()
    for first, second in zip(inward, outward):
        first.wait()
        second.start()
    for copy in outward:
        copy.wait()


def join(keys, queries):
    spec = pl.BlockSpec(memory_space=pl.ANY)
    return pl.pallas_call(
        join_kernel,
        out_shape=shape((16, 32, 2 * N)),
        in_specs=[spec, spec],
        out_specs=spec,
        scratch_shapes=[pltpu.VMEM((2, 16, 16, 2 * N), BF16), pltpu.SemaphoreType.DMA((4,))],
    )(keys, queries)


def send_kernel(gq_ref, gk_ref, parts_ref, out_ref):
    total = jnp.sum(parts_ref[...], axis=0)
    high = total.astype(BF16).astype(F32)
    middle = (total - high).astype(BF16).astype(F32)
    low = total - high - middle
    rows = lax.broadcasted_iota(jnp.int32, (16, N), 0)
    pieces = jnp.where(rows == 0, high, jnp.where(rows == 1, middle, jnp.where(rows == 2, low, 0.0)))
    for at, ref in ((0, gq_ref), (32, gk_ref)):
        out_ref[:, at : at + 16, :] = ref[:, :, :N]
        out_ref[:, at + 16 : at + 32, :] = ref[:, :, N:]
    out_ref[:, 64:, :] = jnp.broadcast_to(pieces.astype(BF16)[None], (16, 16, N))


def receive_kernel(back_ref, gq_ref, gk_ref, square_ref):
    for at, ref in ((0, gq_ref), (32, gk_ref)):
        ref[:, :, :N] = back_ref[:, at : at + 16, :]
        ref[:, :, N:] = back_ref[:, at + 16 : at + 32, :]
    pieces = jnp.sum(back_ref[:, 64:, :].astype(F32), axis=0)
    total = jnp.sum(pieces, axis=0, keepdims=True)
    square_ref[...] = total[:, :1] * (1.0 / (8192 * 16 * (2 * K + V)))


def call(kernel, outs, args, flops, scratch=(), scalars=0):
    spec = pl.BlockSpec(memory_space=pltpu.VMEM)
    smem = pl.BlockSpec(memory_space=pltpu.SMEM)
    moved = sum(a.size * a.dtype.itemsize for a in args)
    return pl.pallas_call(
        kernel,
        out_shape=outs,
        in_specs=[smem] * scalars + [spec] * (len(args) - scalars),
        out_specs=[spec] * len(outs),
        scratch_shapes=list(scratch),
        cost_estimate=pl.CostEstimate(flops=flops, bytes_accessed=moved, transcendentals=0),
        compiler_params=pltpu.CompilerParams(vmem_limit_bytes=24 * 2**20),
    )(*args)


def shape(dims, dtype=BF16):
    return jax.ShapeDtypeStruct(dims, dtype)


def to_heads(array):
    return lax.all_to_all(array, "key", 0, 0, tiled=True)


def local(query_rows, key_rows, value_rows, out_grad, log_gates, write_rate, group_inverse, states):
    keys = jnp.transpose(key_rows, (1, 2, 0))
    queries = jnp.transpose(query_rows, (1, 2, 0))
    kq = to_heads(join(keys, queries))
    grad = out_grad.reshape(2 * N, V)
    values = value_rows.reshape(2 * N, V)
    x, y, c = (lax.axis_index(name) for name in SEQ)
    place = jnp.stack([c, y, x]).astype(jnp.int32)
    chip_map = shape((K + PAD, K + HALF))
    square = shape((K, V), F32)
    basics = (kq, grad, log_gates, write_rate, group_inverse)

    device_map, written_t, local_grad, later_m, later_b = call(
        local_map_kernel,
        [shape((K + PAD, K + V)), shape((K, 2 * N)), square, shape((K, K)), square],
        basics,
        10**8,
    )
    state_blocks, device_map = lax.optimization_barrier((jnp.transpose(states, (1, 0, 2, 3)), device_map))
    state_heads = to_heads(state_blocks)
    chip_other = lax.ppermute(device_map, "c", [(0, 1), (1, 0)])
    (now,) = call(pair_kernel, [chip_map], (place, device_map, chip_other), HIDING, scalars=1)
    plane_half, plane_b, end, end_b = call(
        plane_kernel,
        [shape((ROWS, 2 * HALF)), shape((K, HALF)), shape((K + 8, K), F32), shape((K, HALF))],
        (place, lax.all_gather(now, "y")),
        10**8,
        scalars=1,
    )
    later = [lax.ppermute(plane_half, "x", pairs) for pairs in ([(1, 0), (2, 1), (3, 2)], [(2, 0)])]
    later += [lax.ppermute(plane_b, "x", pairs) for pairs in ([(3, 1)], [(3, 0)])]

    gq, fresh, score_term, query_sum = call(
        ahead_kernel,
        [shape((16, 16, 2 * N)), shape((2 * N, V)), square, shape((8, 128), F32)],
        (*basics, written_t, values, state_heads),
        2 * 10**8,
    )
    later, fresh = lax.optimization_barrier((later, fresh))
    last = jnp.concatenate([later[2] + later[3], end_b], axis=1)
    halves = lax.all_gather(jnp.concatenate([later[0], later[1], last], axis=0), "c")
    gk, grad_value, total = call(
        final_kernel,
        [shape((16, 16, 2 * N)), shape((2 * N, V)), shape((32, 1, 128), F32)],
        (
            place, halves, end, chip_other, later_m, later_b, kq, log_gates, write_rate, group_inverse, local_grad,
            state_heads, fresh, score_term, query_sum,
        ),
        4 * 10**8,
        scalars=1,
    )
    parts = lax.all_to_all(total, SEQ, 0, 0, tiled=True)
    (sent,) = call(send_kernel, [shape((16, 80, N))], (gq, gk, parts), 10**6)
    grad_query, grad_key, grad_square = call(
        receive_kernel,
        [shape((16, 16, 2 * N)), shape((16, 16, 2 * N)), shape((1, 1), F32)],
        (to_heads(sent),),
        10**6,
    )
    return (
        jnp.transpose(grad_query, (2, 0, 1)),
        jnp.transpose(grad_key, (2, 0, 1)),
        grad_value.reshape(2 * N, 1, V),
        grad_square.reshape(()),
    )


def solution(mesh):
    grid = Mesh(mesh.devices.reshape(4, 4, 2, 16), ("x", "y", "c", "key"))
    in_specs = (
        P(SEQ, None, "key"),
        P(SEQ, None, "key"),
        P(SEQ, "key", None),
        P(SEQ, "key", None),
        P("key", SEQ),
        P("key", SEQ),
        P(SEQ, "key", None, None),
        P(SEQ, None, "key", None),
    )
    out_specs = (P(SEQ, None, "key"), P(SEQ, None, "key"), P(SEQ, "key", None), P())
    return jax.shard_map(local, mesh=grid, in_specs=in_specs, out_specs=out_specs, check_vma=False)
```

```python
import jax
import jax.numpy as jnp
from jax import lax
from jax.experimental import pallas as pl
from jax.experimental.pallas import tpu as pltpu
from jax.sharding import Mesh, PartitionSpec as P

F32 = jnp.float32
BF16 = jnp.bfloat16
SEQ = ("x", "y", "c")
N = 128
K = 256
V = 256
HALF = V // 2
PAD = 16
ROWS = K + PAD
HIDING = 6 * 10**10


def nn(a, b):
    return lax.dot_general(a, b, (((1,), (0,)), ((), ())), preferred_element_type=F32)


def nt(a, b):
    return lax.dot_general(a, b, (((1,), (1,)), ((), ())), preferred_element_type=F32)


def tn(a, b):
    return lax.dot_general(a, b, (((0,), (0,)), ((), ())), preferred_element_type=F32)


def split(a):
    high = a.astype(BF16)
    return high, (a - high.astype(F32)).astype(BF16)


def nn2(a, b):
    high, low = split(b)
    return nn(a, high) + nn(a, low)


def tn2(a, b):
    high, low = split(b)
    return tn(a, high) + tn(a, low)


def gates_of(gate_row, rate_row):
    rows = lax.broadcasted_iota(jnp.int32, (N, N), 0)
    cols = lax.broadcasted_iota(jnp.int32, (N, N), 1)
    lower = cols <= rows
    eye = cols == rows
    gate_col = jnp.sum(jnp.where(eye, gate_row, 0.0), axis=1, keepdims=True)
    rate_col = jnp.sum(jnp.where(eye, rate_row, 0.0), axis=1, keepdims=True)
    gamma_col = jnp.sum(jnp.where(lower, gate_row, 0.0), axis=1, keepdims=True)
    gamma_row = jnp.sum(jnp.where(rows <= cols, gate_col, 0.0), axis=0, keepdims=True)
    gamma_end = jnp.sum(gate_row, axis=1, keepdims=True)
    spread = jnp.where(lower, gamma_col - gamma_row, 0.0)
    mask = jnp.where(lower, jnp.exp(spread), 0.0)
    return gamma_row, gamma_end, mask, rate_col


def compose(first, second):
    decay1, m1, b1 = first
    decay2, m2, b2 = second
    both = nn(m1.astype(BF16), jnp.concatenate([m2, b2], axis=1).astype(BF16))
    return decay1 * decay2, decay2 * m1 + decay1 * m2 - both[:, :K], decay1 * b2 + b1 - both[:, K:]


def apply(first, state):
    decay, m, b = first
    return decay * state + b - nn(m.astype(BF16), state.astype(BF16))


def decay_rows(decay, width):
    high = decay.astype(BF16).astype(F32)
    middle = (decay - high).astype(BF16).astype(F32)
    low = decay - high - middle
    rows = lax.broadcasted_iota(jnp.int32, (PAD, width), 0)
    return jnp.where(rows == 0, high, jnp.where(rows == 1, middle, jnp.where(rows == 2, low, 0.0))).astype(BF16)


def decay_from(block):
    return jnp.sum(block.astype(F32), axis=0, keepdims=True)[:, :1]


def unpack(block):
    return decay_from(block[K:]), block[:K, :K].astype(F32), block[:K, K:].astype(F32)


def pack(ref, decayed):
    decay, m, b = decayed
    ref[:K, :K] = m.astype(BF16)
    ref[:K, K:] = b.astype(BF16)
    ref[K:, :] = decay_rows(decay, ref.shape[1])


def choose(flag, if_set, if_not):
    return tuple(jnp.where(flag, p, q) for p, q in zip(if_set, if_not))


def head_rows(kq_ref, which):
    return kq_ref[:, 16 * which : 16 * which + 16, :].reshape(K, 2 * N)


def local_map_kernel(kq_ref, grad_ref, gate_ref, rate_ref, inv_ref, map_ref, wt_ref, lg_ref, later_m_ref, later_b_ref):
    key_t = head_rows(kq_ref, 0)
    query_t = head_rows(kq_ref, 1)
    maps = []
    for g in range(2):
        span = slice(g * N, (g + 1) * N)
        rate = rate_ref[:, span]
        gamma, gamma_end, mask, _ = gates_of(gate_ref[:, span], rate)
        kt, qt = key_t[:, span], query_t[:, span]
        into = jnp.exp(gamma)
        scaled = (kt * (rate * into)).astype(BF16)
        wt = nt(scaled, inv_ref[g, 0]).astype(BF16)
        wt_ref[:, span] = wt
        score = (tn(qt, kt) * mask).astype(BF16)
        out_t = (kt * jnp.exp(gamma_end - gamma)).astype(BF16)
        in_t = (qt * into).astype(BF16)
        grad = grad_ref[span, :]
        lg = tn(score, grad)
        lg_ref[span, :] = lg
        offset = nn(in_t, grad) - nn2(wt, lg)
        maps.append((jnp.exp(gamma_end), nt(wt, out_t), offset))
    pack(map_ref, compose(*maps))
    later_m_ref[...] = maps[1][1].astype(BF16)
    later_b_ref[...] = maps[1][2]


def pair_kernel(place_ref, own_ref, other_ref, map_ref):
    upper = place_ref[0] == 1

    def half(ref):
        decay, m, b = unpack(ref[...])
        return decay, m, jnp.where(upper, b[:, HALF:], b[:, :HALF])

    own, other = half(own_ref), half(other_ref)
    pack(map_ref, compose(choose(upper, other, own), choose(upper, own, other)))


def plane_kernel(place_ref, chips_ref, send_ref, send_b_ref, end_ref, end_b_ref):
    suffix = unpack(chips_ref[3])
    end = (jnp.ones((1, 1), F32), jnp.zeros((K, K), F32), jnp.zeros((K, HALF), F32))
    for j in (2, 1, 0):
        end = choose(place_ref[1] == j, suffix, end)
        suffix = compose(unpack(chips_ref[j]), suffix)
    decay, m, b = suffix
    m_half = jnp.where(place_ref[0] == 0, m[:, :HALF], m[:, HALF:])
    send_ref[:K, :HALF] = m_half.astype(BF16)
    send_ref[:K, HALF:] = b.astype(BF16)
    send_ref[K:, :] = decay_rows(decay, 2 * HALF)
    send_b_ref[...] = b.astype(BF16)
    decay, m, b = end
    end_ref[:K, :] = m
    end_ref[K:, :] = jnp.broadcast_to(decay, (8, K))
    end_b_ref[...] = b.astype(BF16)


def ahead_kernel(kq_ref, grad_ref, gate_ref, rate_ref, inv_ref, wt_ref, value_ref, state_ref,
                 gq_ref, nv_ref, ct_ref, sum_ref):
    key_t = head_rows(kq_ref, 0)
    query_t = head_rows(kq_ref, 1)
    total = jnp.zeros((1, 1), F32)
    for g in range(2):
        span = slice(g * N, (g + 1) * N)
        gamma, _, mask, rate_col = gates_of(gate_ref[:, span], rate_ref[:, span])
        kt, qt = key_t[:, span], query_t[:, span]
        state = state_ref[:, g].reshape(K, V)
        grad = grad_ref[span, :]
        scaled = (value_ref[span, :] * rate_col).astype(BF16)
        fresh = (nn(inv_ref[g, 0], scaled) - tn(wt_ref[:, span], state)).astype(BF16)
        nv_ref[span, :] = fresh
        score = (nt(grad, fresh) * mask).astype(BF16)
        gq = (jnp.exp(gamma) * nt(state, grad) + nt(kt, score)).astype(BF16)
        gq_ref[:, :, span] = gq.reshape(16, 16, N)
        ct_ref[:, span] = nn(qt, score)
        total += jnp.sum(jnp.square(gq.astype(F32)), keepdims=True)
    sum_ref[...] = jnp.broadcast_to(total, (8, 128))


def state_after(place_ref, halves_ref, end_ref, other_ref):
    low, high = (halves_ref[i, 2 * ROWS :, :].astype(F32) for i in range(2))
    state = jnp.concatenate([low[:, :HALF], high[:, :HALF]], axis=1)
    end_b = jnp.concatenate([low[:, HALF:], high[:, HALF:]], axis=1)
    for d in (1, 0):
        low, high = (halves_ref[i, ROWS * (1 - d) : ROWS * (2 - d), :] for i in range(2))
        m = jnp.concatenate([low[:K, :HALF], high[:K, :HALF]], axis=1)
        b = jnp.concatenate([low[:K, HALF:], high[:K, HALF:]], axis=1).astype(F32)
        ahead = apply((decay_from(low[K:]), m, b), state)
        state = jnp.where(place_ref[2] == 1, state, ahead) if d == 1 else ahead
    state = apply((end_ref[K : K + 1, :1], end_ref[:K, :], end_b), state)
    return jnp.where(place_ref[0] == 0, apply(unpack(other_ref[...]), state), state)


def final_kernel(place_ref, halves_ref, end_ref, other_ref, later_m_ref, later_b_ref, kq_ref, gate_ref, rate_ref,
                 inv_ref, lg_ref, state_ref, nv_ref, ct_ref, sum_ref, gk_ref, gv_ref, total_ref):
    key_t = head_rows(kq_ref, 0)
    state_grad = state_after(place_ref, halves_ref, end_ref, other_ref)
    total = sum_ref[:1, :1]
    for g in (1, 0):
        span = slice(g * N, (g + 1) * N)
        rate = rate_ref[:, span]
        gamma, gamma_end, _, rate_col = gates_of(gate_ref[:, span], rate)
        into = jnp.exp(gamma)
        away = jnp.exp(gamma_end - gamma)
        inverse = inv_ref[g, 0]
        out_t = (key_t[:, span] * away).astype(BF16)
        high, low = split(state_grad)
        value_grad = lg_ref[span, :] + tn(out_t, high) + tn(out_t, low)
        rounded = value_grad.astype(BF16)
        gv = (rate_col * tn(inverse, rounded)).astype(BF16)
        gv_ref[span, :] = gv
        write_t = (-nt(state_ref[:, g].reshape(K, V), rounded)).astype(BF16)
        gk = (ct_ref[:, span] + away * nt(high, nv_ref[span, :]) + (rate * into) * nn(write_t, inverse)).astype(BF16)
        gk_ref[:, :, span] = gk.reshape(16, 16, N)
        total += jnp.sum(jnp.square(gk.astype(F32)), keepdims=True) + jnp.sum(
            jnp.square(gv.astype(F32)), keepdims=True
        )
        if g == 1:
            state_grad = apply((jnp.exp(gamma_end), later_m_ref[...], later_b_ref[...]), state_grad)
    total_ref[...] = jnp.broadcast_to(total[None], (32, 1, 128))


def join_kernel(key_ref, query_ref, out_ref, held, done):
    inward = [pltpu.make_async_copy(ref, held.at[i], done.at[i]) for i, ref in enumerate((key_ref, query_ref))]
    outward = [
        pltpu.make_async_copy(held.at[i], out_ref.at[:, pl.ds(16 * i, 16), :], done.at[2 + i]) for i in range(2)
    ]
    for copy in inward:
        copy.start()
    for first, second in zip(inward, outward):
        first.wait()
        second.start()
    for copy in outward:
        copy.wait()


def join(keys, queries):
    spec = pl.BlockSpec(memory_space=pl.ANY)
    return pl.pallas_call(
        join_kernel,
        out_shape=shape((16, 32, 2 * N)),
        in_specs=[spec, spec],
        out_specs=spec,
        scratch_shapes=[pltpu.VMEM((2, 16, 16, 2 * N), BF16), pltpu.SemaphoreType.DMA((4,))],
    )(keys, queries)


def send_kernel(gq_ref, gk_ref, parts_ref, out_ref):
    total = jnp.sum(parts_ref[...], axis=0)
    high = total.astype(BF16).astype(F32)
    middle = (total - high).astype(BF16).astype(F32)
    low = total - high - middle
    rows = lax.broadcasted_iota(jnp.int32, (16, N), 0)
    pieces = jnp.where(rows == 0, high, jnp.where(rows == 1, middle, jnp.where(rows == 2, low, 0.0)))
    for at, ref in ((0, gq_ref), (32, gk_ref)):
        out_ref[:, at : at + 16, :] = ref[:, :, :N]
        out_ref[:, at + 16 : at + 32, :] = ref[:, :, N:]
    out_ref[:, 64:, :] = jnp.broadcast_to(pieces.astype(BF16)[None], (16, 16, N))


def receive_kernel(back_ref, gq_ref, gk_ref, square_ref):
    for at, ref in ((0, gq_ref), (32, gk_ref)):
        ref[:, :, :N] = back_ref[:, at : at + 16, :]
        ref[:, :, N:] = back_ref[:, at + 16 : at + 32, :]
    pieces = jnp.sum(back_ref[:, 64:, :].astype(F32), axis=0)
    total = jnp.sum(pieces, axis=0, keepdims=True)
    square_ref[...] = total[:, :1] * (1.0 / (8192 * 16 * (2 * K + V)))


def call(kernel, outs, args, flops, scratch=(), scalars=0):
    spec = pl.BlockSpec(memory_space=pltpu.VMEM)
    smem = pl.BlockSpec(memory_space=pltpu.SMEM)
    moved = sum(a.size * a.dtype.itemsize for a in args)
    return pl.pallas_call(
        kernel,
        out_shape=outs,
        in_specs=[smem] * scalars + [spec] * (len(args) - scalars),
        out_specs=[spec] * len(outs),
        scratch_shapes=list(scratch),
        cost_estimate=pl.CostEstimate(flops=flops, bytes_accessed=moved, transcendentals=0),
        compiler_params=pltpu.CompilerParams(vmem_limit_bytes=24 * 2**20),
    )(*args)


def shape(dims, dtype=BF16):
    return jax.ShapeDtypeStruct(dims, dtype)


def to_heads(array):
    return lax.all_to_all(array, "key", 0, 0, tiled=True)


def local(query_rows, key_rows, value_rows, out_grad, log_gates, write_rate, group_inverse, states):
    keys = jnp.transpose(key_rows, (1, 2, 0))
    queries = jnp.transpose(query_rows, (1, 2, 0))
    kq = to_heads(join(keys, queries))
    grad = out_grad.reshape(2 * N, V)
    values = value_rows.reshape(2 * N, V)
    x, y, c = (lax.axis_index(name) for name in SEQ)
    place = jnp.stack([c, y, x]).astype(jnp.int32)
    chip_map = shape((K + PAD, K + HALF))
    square = shape((K, V), F32)
    basics = (kq, grad, log_gates, write_rate, group_inverse)

    device_map, written_t, local_grad, later_m, later_b = call(
        local_map_kernel,
        [shape((K + PAD, K + V)), shape((K, 2 * N)), square, shape((K, K)), square],
        basics,
        10**8,
    )
    state_blocks, device_map = lax.optimization_barrier((jnp.transpose(states, (1, 0, 2, 3)), device_map))
    state_heads = to_heads(state_blocks)
    chip_other = lax.ppermute(device_map, "c", [(0, 1), (1, 0)])
    (now,) = call(pair_kernel, [chip_map], (place, device_map, chip_other), HIDING, scalars=1)
    plane_half, plane_b, end, end_b = call(
        plane_kernel,
        [shape((ROWS, 2 * HALF)), shape((K, HALF)), shape((K + 8, K), F32), shape((K, HALF))],
        (place, lax.all_gather(now, "y")),
        10**8,
        scalars=1,
    )
    two_ahead = lax.ppermute(plane_half, "x", [(2, 0)])
    later = [two_ahead, lax.ppermute(plane_half, "x", [(1, 0), (2, 1), (3, 2)])]
    later += [lax.ppermute(plane_b, "x", pairs) for pairs in ([(3, 1)], [(3, 0)])]

    gq, fresh, score_term, query_sum = call(
        ahead_kernel,
        [shape((16, 16, 2 * N)), shape((2 * N, V)), square, shape((8, 128), F32)],
        (*basics, written_t, values, state_heads),
        2 * 10**8,
    )
    later, fresh = lax.optimization_barrier((later, fresh))
    last = jnp.concatenate([later[2] + later[3], end_b], axis=1)
    halves = lax.all_gather(jnp.concatenate([later[0], later[1], last], axis=0), "c")
    gk, grad_value, total = call(
        final_kernel,
        [shape((16, 16, 2 * N)), shape((2 * N, V)), shape((32, 1, 128), F32)],
        (
            place, halves, end, chip_other, later_m, later_b, kq, log_gates, write_rate, group_inverse, local_grad,
            state_heads, fresh, score_term, query_sum,
        ),
        4 * 10**8,
        scalars=1,
    )
    parts = lax.all_to_all(total, SEQ, 0, 0, tiled=True)
    (sent,) = call(send_kernel, [shape((16, 80, N))], (gq, gk, parts), 10**6)
    grad_query, grad_key, grad_square = call(
        receive_kernel,
        [shape((16, 16, 2 * N)), shape((16, 16, 2 * N)), shape((1, 1), F32)],
        (to_heads(sent),),
        10**6,
    )
    return (
        jnp.transpose(grad_query, (2, 0, 1)),
        jnp.transpose(grad_key, (2, 0, 1)),
        grad_value.reshape(2 * N, 1, V),
        grad_square.reshape(()),
    )


def solution(mesh):
    grid = Mesh(mesh.devices.reshape(4, 4, 2, 16), ("x", "y", "c", "key"))
    in_specs = (
        P(SEQ, None, "key"),
        P(SEQ, None, "key"),
        P(SEQ, "key", None),
        P(SEQ, "key", None),
        P("key", SEQ),
        P("key", SEQ),
        P(SEQ, "key", None, None),
        P(SEQ, None, "key", None),
    )
    out_specs = (P(SEQ, None, "key"), P(SEQ, None, "key"), P(SEQ, "key", None), P())
    return jax.shard_map(local, mesh=grid, in_specs=in_specs, out_specs=out_specs, check_vma=False)
```
